256 devices in a mesh: cell: 2 (over core), bini: 16 (over y, x), binj: 8 (over z).
Axes of the slice: x: 4, y: 4, z: 8, core: 2. Of those that a mesh axis runs over, the one named last changes fastest.
Arguments:
- contacts: float32 [32, 3072, 3072], P('cell', 'bini', 'binj'), may hold values from -49 to 49
- first_bins: float32 [24, 3072], P(None, ('bini', 'cell', 'binj')), may hold values from -24 to 24
- second_bins: float32 [24, 3072], P(None, ('binj', 'cell', 'bini')), may hold values from -24 to 24
Outputs:
- cell_factor: float32 [24, 32], P(None, 'cell')
- first_factor: float32 [24, 3072], P(None, ('bini', 'cell', 'binj'))
- second_factor: float32 [24, 3072], P(None, ('binj', 'cell', 'bini'))
The draws below stay inside these ranges and needn't reach their ends.
All inputs are finite; a program needn't handle non-finite values.
Results may differ from the reference program's by a relative error of at most 0.0002.
Values sent between devices are 32-bit elements; how exact they have to be, the bound alone decides.
A program may use at most 64 MiB of HBM per device.

```python
import math
import jax
import jax.numpy as jnp
from jax import lax

R = 24
J = 3072
K = 3072
SWEEPS = 1
I = 32


def draw_contacts(key, part):
    key = jax.random.fold_in(key, 5)
    key_noise, key_level = jax.random.split(key, 2)
    rise_first = 0.6 + 1.2 * jnp.arange(J, dtype=jnp.float32) / J
    rise_second = 0.6 + 1.2 * jnp.arange(K, dtype=jnp.float32) / K
    noise_draw = jnp.clip(jax.random.normal(key_noise, (I, J, K), jnp.float32), -5.0, 5.0)
    level_draw = jnp.exp(jax.random.uniform(key_level, (I,), jnp.float32, 0.0, math.log(3.0)))
    values = noise_draw * level_draw[:, None, None] * rise_first[None, :, None] * rise_second[None, None, :]
    return values.astype(jnp.float32)


def draw_first_bins(key, part):
    key = jax.random.fold_in(key, 11)
    key_noise, key_shared, key_rough = jax.random.split(key, 3)
    rise_rows = 0.6 + 1.2 * jnp.arange(J, dtype=jnp.float32) / J
    noise_draw = jnp.clip(jax.random.normal(key_noise, (R, J), jnp.float32), -4.0, 4.0)
    shared_draw = jnp.clip(jax.random.normal(key_shared, (J,), jnp.float32), -4.0, 4.0)
    rough_draw = jnp.exp(math.log(10.0) * jax.random.uniform(key_rough, (J,), jnp.float32))
    values = (rise_rows * rough_draw)[None, :] * (noise_draw + shared_draw[None, :]) / 6.0
    return values.astype(jnp.float32)


def draw_second_bins(key, part):
    key = jax.random.fold_in(key, 23)
    key_noise, key_shared, key_rough = jax.random.split(key, 3)
    rise_rows = 0.6 + 1.2 * jnp.arange(K, dtype=jnp.float32) / K
    noise_draw = jnp.clip(jax.random.normal(key_noise, (R, K), jnp.float32), -4.0, 4.0)
    shared_draw = jnp.clip(jax.random.normal(key_shared, (K,), jnp.float32), -4.0, 4.0)
    rough_draw = jnp.exp(math.log(10.0) * jax.random.uniform(key_rough, (K,), jnp.float32))
    values = (rise_rows * rough_draw)[None, :] * (noise_draw + shared_draw[None, :]) / 6.0
    return values.astype(jnp.float32)


def setup_inputs(seed: int = 0) -> dict:
    keys = jax.random.split(jax.random.key(seed), 4)
    return {
        "contacts": draw_contacts(jax.random.fold_in(keys[3], 71), 0),
        "first_bins": draw_first_bins(jax.random.fold_in(keys[3], 71), 0),
        "second_bins": draw_second_bins(jax.random.fold_in(keys[3], 71), 0),
    }


EPSILON = 1e-06
PRECISE = lax.Precision.HIGHEST

def gram_of(factor):
    return jnp.dot(factor.astype(jnp.float32), factor.T.astype(jnp.float32), precision=PRECISE, preferred_element_type=jnp.float32)

def normal_solve(system, right_terms):
    factor_low = jnp.linalg.cholesky(system)
    midway = lax.linalg.triangular_solve(factor_low, right_terms, left_side=True, lower=True)
    return lax.linalg.triangular_solve(factor_low, midway, left_side=True, lower=True, transpose_a=True)

def rescale(unscaled, unscaled_gram, row_total):
    column_scale = jnp.sqrt(jnp.diagonal(unscaled_gram) / row_total + EPSILON)
    return (unscaled / column_scale[:, None], unscaled_gram / (column_scale[:, None] * column_scale[None, :]))

def reference(contacts, first_bins, second_bins):
    first_now = first_bins
    second_now = second_bins
    gram_first = gram_of(first_now)
    gram_second = gram_of(second_now)
    cell_factor = jnp.zeros((R, I), jnp.float32)
    for sweep_index in range(SWEEPS):

        def along_second(cell_plane, second_used=second_now):
            return lax.dot_general(second_used.astype(jnp.float32), cell_plane.astype(jnp.float32), (((1,), (1,)), ((), ())), precision=PRECISE, preferred_element_type=jnp.float32)
        partial_first = lax.map(along_second, contacts)
        cell_terms = lax.optimization_barrier(jnp.sum(partial_first * first_now[None, :, :], axis=2)).T
        unscaled = normal_solve(gram_first * gram_second, cell_terms)
        cell_factor, gram_cells = rescale(unscaled, gram_of(unscaled), I)
        first_terms = lax.optimization_barrier(jnp.sum(partial_first * cell_factor.T[:, :, None], axis=0))
        unscaled = normal_solve(gram_cells * gram_second, first_terms)
        first_now, gram_first = rescale(unscaled, gram_of(unscaled), J)

        def along_first(cell_plane, first_used=first_now):
            return lax.dot_general(first_used.astype(jnp.float32), cell_plane.astype(jnp.float32), (((1,), (0,)), ((), ())), precision=PRECISE, preferred_element_type=jnp.float32)
        partial_second = lax.map(along_first, contacts)
        second_terms = lax.optimization_barrier(jnp.sum(partial_second * cell_factor.T[:, :, None], axis=0))
        unscaled = normal_solve(gram_cells * gram_first, second_terms)
        second_now, gram_second = rescale(unscaled, gram_of(unscaled), K)
    return (cell_factor, first_now, second_now)
```

```python
import functools

import jax
import jax.numpy as jnp
from jax import lax
from jax.experimental import pallas as pl
from jax.experimental.pallas import tpu as pltpu
from jax.sharding import PartitionSpec as P

EPSILON = 1e-06
PRECISE = lax.Precision.HIGHEST
MESH = pl.DeviceIdType.MESH
R = 24
G = 3
SPREAD = 40
NT = (((1,), (1,)), ((), ()))


def lanes(shape):
    return lax.broadcasted_iota(jnp.int32, shape, 1)


def group(value, q):
    return value[8 * q : 8 * q + 8, :]


def stack(tiles):
    return jnp.concatenate(tiles, axis=0)


def turn(value, shift):
    if isinstance(shift, int):
        shift = shift % 128
        return value if shift == 0 else pltpu.roll(value, shift, 1)
    return pltpu.roll(value, shift, 1)


def pack(value, step, base=None):
    out = None
    for q in range(G):
        if base is None:
            tile = turn(group(value, q), step * q)
        else:
            tile = turn(group(value, q), lax.rem(base + step * q, 128))
        out = tile if out is None else out + tile
    return out


def unpack(tile, step, width, base=None):
    parts = []
    for q in range(G):
        if base is None:
            part = turn(tile, -step * q)
        else:
            part = turn(tile, lax.rem(256 - base - step * q, 128))
        parts.append(jnp.where(lanes(part.shape) < width, part, 0.0))
    return stack(parts)


def within(lane, start, width):
    return ((lane - start) & 127) < width


def spread(tile_at, count, width, tiles):
    lane = lanes((8, 128))
    out = [[jnp.zeros((8, 128), jnp.float32) for _ in range(tiles)] for _ in range(G)]
    for o in range(count):
        tile = tile_at(o)
        start = width * o
        for t in range(tiles):
            low, high = max(start, 128 * t), min(start + width, 128 * t + 128)
            if low >= high:
                continue
            for q in range(G):
                mask = within(lane, (low + SPREAD * q) % 128, high - low)
                out[q][t] = jnp.where(mask, tile, out[q][t])
    return [stack([turn(out[q][t], -SPREAD * q) for q in range(G)]) for t in range(tiles)]


def owner_tiles(tiles, count, width):
    lane = lanes((8, 128))
    moved = [[turn(group(tile, q), SPREAD * q) for tile in tiles] for q in range(G)]
    out = []
    for o in range(count):
        start = width * o
        packed = None
        for q in range(G):
            for t in range(len(tiles)):
                low, high = max(start, 128 * t), min(start + width, 128 * t + 128)
                if low >= high:
                    continue
                if packed is None:
                    packed = moved[q][t]
                else:
                    packed = jnp.where(within(lane, (low + SPREAD * q) % 128, high - low), moved[q][t], packed)
        out.append(packed)
    return out


def split(value):
    high = value.astype(jnp.bfloat16)
    return high, (value - high.astype(jnp.float32)).astype(jnp.bfloat16)


def split_rows(value):
    high = value.astype(jnp.bfloat16).astype(jnp.float32)
    return jnp.concatenate([high, value - high], axis=0).astype(jnp.bfloat16)


def gram(tiles):
    total = None
    for tile in tiles:
        tall = jnp.concatenate([tile, jnp.zeros((128 - R, 128), jnp.float32)], axis=0)
        part = lax.dot_general(tile, tall, NT, precision=PRECISE, preferred_element_type=jnp.float32)
        total = part if total is None else total + part
    return total


def inverse(a):
    lane, row = lanes((R, 128)), lax.broadcasted_iota(jnp.int32, (R, 128), 0)
    for k in range(R):
        pivot_row = a[k : k + 1, :]
        pivot_column = a[:, k : k + 1]
        over = 1.0 / a[k : k + 1, k : k + 1]
        new_row = jnp.where(lane[:1] == k, over, pivot_row * over)
        a = jnp.where(lane == k, 0.0, a) - pivot_column * new_row
        a = jnp.where(row == k, new_row, a)
    return a


def apply(matrix, value):
    total = None
    for s in range(R):
        term = matrix[:, s : s + 1] * value[s : s + 1, :]
        total = term if total is None else total + term
    return total


def diagonal_scales(raw, count):
    lane, row = lanes((R, 128)), lax.broadcasted_iota(jnp.int32, (R, 128), 0)
    diagonal = jnp.where(lane == row, raw, 0.0)
    column = jnp.sum(diagonal, axis=1, keepdims=True)
    across = jnp.sum(diagonal, axis=0, keepdims=True)
    return jnp.sqrt(column / count + EPSILON), jnp.sqrt(across / count + EPSILON)


def kernel(
    sizes,
    contacts,
    first_in,
    second_in,
    cell_out,
    first_out,
    second_out,
    x_full,
    x_high,
    x_low,
    first_land,
    second_land,
    first_pad,
    second_pad,
    first_slots,
    second_slots,
    terms_z,
    grams_xy,
    terms_xy,
    products,
    halves,
    half_in,
    halves_z,
    solved,
    raw_xy,
    owned_out,
    owned_in,
    norms_xy,
    norms_z,
    load_sem,
    send_sem,
    recv_sem,
):
    C, A, B, I, J, K = sizes
    cells, rows = x_full.shape[0], x_full.shape[1]
    width_first, width_second = rows // (C * B), x_full.shape[2] // (C * A)
    c, a, b = lax.axis_index("cell"), lax.axis_index("bini"), lax.axis_index("binj")
    in_cz, in_cxy = c * B + b, c * A + a
    other = (1 - c, a, b)
    lane8, lane24 = lanes((8, 128)), lanes((R, 128))

    loads = [
        pltpu.make_async_copy(second_in, second_land, load_sem.at[0]),
        pltpu.make_async_copy(first_in, first_land, load_sem.at[1]),
    ]
    for load in loads:
        load.start()

    def load_cell(i):
        return pltpu.make_async_copy(contacts.at[i], x_full.at[i], load_sem.at[2 + i])

    for i in range(cells):
        load_cell(i).start()

    barrier = pltpu.get_barrier_semaphore()

    def signal(device):
        pl.semaphore_signal(barrier, inc=1, device_id=device, device_id_type=MESH)

    def z_partner(k):
        return (c, a, lax.rem(b + k, B))

    def xy_partner(k):
        return (c, lax.rem(a + k, A), b)

    def cz_partner(k):
        return (lax.rem(c + k // B, C), a, lax.rem(b + lax.rem(k, B), B))

    def cxy_partner(k):
        return (lax.rem(c + k // A, C), lax.rem(a + lax.rem(k, A), A), b)

    def greet_cz(k, carry):
        signal(cz_partner(k))
        return carry

    def greet_cxy(k, carry):
        signal(cxy_partner(k))
        return carry

    lax.fori_loop(1, C * B, greet_cz, 0)
    lax.fori_loop(1, A, greet_cxy, 0)
    lax.fori_loop(A + 1, C * A, greet_cxy, 0)

    second_pad[...] = jnp.zeros_like(second_pad)
    first_pad[...] = jnp.zeros_like(first_pad)
    loads[0].wait()
    second_pad[:, :width_second] = second_land[...]
    loads[1].wait()
    first_pad[:, :width_first] = first_land[...]
    second_slots[in_cxy] = pack(second_pad[...], SPREAD, lax.rem(width_second * in_cxy, 128))
    first_slots[in_cz] = pack(first_pad[...], SPREAD, lax.rem(width_first * in_cz, 128))

    def send(source, target, number, device):
        pltpu.make_async_remote_copy(
            source, target, send_sem.at[number], recv_sem.at[number], device_id=device, device_id_type=MESH
        ).start()

    def send_all(source, target, number, partner, count):
        def one(k, carry):
            send(source, target, number, partner(k))
            return carry

        lax.fori_loop(1, count, one, 0)

    def arrived(like, number):
        pltpu.make_async_copy(like, like, recv_sem.at[number]).wait()

    def left(like, number):
        pltpu.make_async_copy(like, like, send_sem.at[number]).wait()

    def split_cell(i, carry):
        load_cell(i).wait()
        high, low = split(x_full[i])
        at = pl.ds(pl.multiple_of(i * rows, rows), rows)
        x_high[at, :] = high
        x_low[at, :] = low
        return carry

    lax.fori_loop(0, cells // 2, split_cell, 0)
    pl.semaphore_wait(barrier, C * B - 1 + C * (A - 1))

    mine = second_slots.at[in_cxy]
    send_all(mine, mine, 0, cxy_partner, C * A)
    mine = first_slots.at[in_cz]
    send_all(mine, mine, 1, cz_partner, C * B)
    lax.fori_loop(cells // 2, cells, split_cell, 0)

    arrived(second_slots.at[pl.ds(0, C * A - 1)], 0)
    second = spread(lambda o: second_slots[o], C * A, width_second, 3)
    second_rows = split_rows(jnp.concatenate(second, axis=1))
    arrived(first_slots.at[pl.ds(0, C * B - 1)], 1)
    first = spread(lambda o: first_slots[o], C * B, width_first, 2)
    first_turned = [turn(group(first[0], q), 64) for q in range(G)]
    first_turned = stack(first_turned)
    last_turned = stack([turn(group(first[1], q), 64) for q in range(G)])
    first_pair = [
        first[0],
        jnp.where(lane24 < 64, first[1], first_turned),
        jnp.where(lane24 < 64, first_turned, last_turned),
    ]

    cell_terms = jnp.zeros((R, 128), jnp.float32)
    for p in range(cells // 2):
        at = pl.ds(2 * rows * p, 2 * rows)
        big = lax.dot_general(second_rows, x_high[at, :], NT, preferred_element_type=jnp.float32)
        small = lax.dot_general(second_rows, x_low[at, :], NT, preferred_element_type=jnp.float32)
        both = (small[:R] + small[R:]) + big[R:] + big[:R]
        products[p] = both
        terms = [both[:, 128 * t : 128 * t + 128] * first_pair[t] for t in range(3)]
        even = jnp.sum(terms[0] + jnp.where(lane24 < 64, terms[1], 0.0), axis=1, keepdims=True)
        odd = jnp.sum(terms[2] + jnp.where(lane24 < 64, 0.0, terms[1]), axis=1, keepdims=True)
        cell_terms = jnp.where(lane24 == 2 * p, even, cell_terms)
        cell_terms = jnp.where(lane24 == 2 * p + 1, odd, cell_terms)

    terms_z[b] = pack(cell_terms, cells) + turn(pack(gram(second), R), 56)
    mine = terms_z.at[b]
    send_all(mine, mine, 2, z_partner, B)
    grams_xy[a] = pack(gram(first), R)
    mine = grams_xy.at[a]
    send_all(mine, mine, 3, xy_partner, A)

    arrived(terms_z.at[pl.ds(0, B - 1)], 2)
    summed = terms_z[0]
    for o in range(1, B):
        summed = summed + terms_z[o]
    terms_xy[in_cxy] = jnp.where(lane8 < G * cells, summed, 0.0)
    mine = terms_xy.at[in_cxy]
    send_all(mine, mine, 4, cxy_partner, C * A)

    gram_second = unpack(turn(summed, -56), R, R)
    arrived(grams_xy.at[pl.ds(0, A - 1)], 3)
    summed = grams_xy[0]
    for o in range(1, A):
        summed = summed + grams_xy[o]
    gram_first = unpack(summed, R, R)
    system = inverse(gram_first * gram_second)

    arrived(terms_xy.at[pl.ds(0, C * A - 1)], 4)
    cell_total = None
    for core in range(C):
        summed = terms_xy[core * A]
        for o in range(1, A):
            summed = summed + terms_xy[core * A + o]
        block = unpack(summed, cells, cells)
        block = stack([turn(group(block, q), cells * core) for q in range(G)])
        cell_total = block if cell_total is None else cell_total + block

    unscaled = apply(system, cell_total)
    scale = jnp.sqrt(jnp.sum(unscaled * unscaled, axis=1, keepdims=True) / I + EPSILON)
    cell_factor = unscaled / scale
    own_cells = stack([turn(group(cell_factor, q), lax.rem(128 - cells * c, 128)) for q in range(G)])
    cell_out[...] = own_cells[:, :cells]

    pair_sum = [jnp.zeros((R, 128), jnp.float32) for _ in range(3)]
    weights = []
    for p in range(cells // 2):
        even = jnp.broadcast_to(own_cells[:, 2 * p : 2 * p + 1], (R, 128))
        odd = jnp.broadcast_to(own_cells[:, 2 * p + 1 : 2 * p + 2], (R, 128))
        weight = [even, jnp.where(lane24 < 64, even, odd), odd]
        weights.append(weight)
        both = products[p]
        for t in range(3):
            pair_sum[t] = pair_sum[t] + both[:, 128 * t : 128 * t + 128] * weight[t]

    def half_turn(value):
        return stack([turn(group(value, q), 64) for q in range(G)])

    turned = [half_turn(pair_sum[1]), half_turn(pair_sum[2])]
    halves[0] = pair_sum[0] + jnp.where(lane24 < 64, turned[0], turned[1])
    halves[1] = jnp.where(lane24 < 64, pair_sum[1] + turned[1], 0.0)
    send(halves.at[1 - c], half_in, 5, other)

    raw = gram([unscaled])
    scale_column, scale_row = diagonal_scales(raw, I)
    gram_cells = jnp.where(lane24 < R, raw / (scale_column * scale_row), 0.0)

    arrived(half_in, 5)
    halves_z[b] = halves[c] + half_in[...]
    mine = halves_z.at[b]
    send_all(mine, mine, 6, z_partner, B)
    system = inverse(gram_cells * gram_second)
    arrived(halves_z.at[pl.ds(0, B - 1)], 6)
    summed = halves_z[0]
    for o in range(1, B):
        summed = summed + halves_z[o]
    solved[c] = apply(system, summed)
    mine = solved.at[c]
    send(mine, mine, 7, other)
    arrived(solved.at[0], 7)
    low, high = solved[0], solved[1]

    low_turned, high_turned = half_turn(low), half_turn(high)
    solved_pair = [
        low,
        jnp.where(lane24 < 64, high, low_turned),
        jnp.where(lane24 < 64, low_turned, high_turned),
    ]
    total = None
    for p in range(cells // 2):
        at = pl.ds(2 * rows * p, 2 * rows)
        left_rows = split_rows(
            jnp.concatenate([solved_pair[t] * weights[p][t] for t in range(3)], axis=1)
        )
        big = jnp.dot(left_rows, x_high[at, :], preferred_element_type=jnp.float32)
        small = jnp.dot(left_rows, x_low[at, :], preferred_element_type=jnp.float32)
        both = big + small
        total = both if total is None else total + both
    total = total[:R] + total[R:]

    tiles = owner_tiles([total[:, 128 * t : 128 * t + 128] for t in range(3)], C * A, width_second)
    for o in range(C * A):
        owned_out[o] = tiles[o]

    def send_owned(k, carry):
        goal = lax.rem(c + k // A, C) * A + lax.rem(a + lax.rem(k, A), A)
        send(owned_out.at[goal], owned_in.at[k - 1], 8, cxy_partner(k))
        return carry

    lax.fori_loop(1, C * A, send_owned, 0)

    raw_xy[a] = pack(gram([low, high]), R)
    mine = raw_xy.at[a]
    send_all(mine, mine, 9, xy_partner, A)
    arrived(raw_xy.at[pl.ds(0, A - 1)], 9)
    summed = raw_xy[0]
    for o in range(1, A):
        summed = summed + raw_xy[o]
    raw = unpack(summed, R, R)
    scale_column, scale_row = diagonal_scales(raw, J)
    gram_first = jnp.where(lane24 < R, raw / (scale_column * scale_row), 0.0)
    system = inverse(gram_cells * gram_first)
    start = width_first * in_cz
    at_low = lax.rem(256 - start, 128)
    piece = stack(
        [
            jnp.where(
                lane8 < 128 - start,
                turn(group(low, q), at_low),
                turn(group(high, q), at_low),
            )
            for q in range(G)
        ]
    )
    first_out[...] = (piece / scale_column)[:, :width_first]

    arrived(owned_in, 8)
    summed = owned_out[in_cxy]
    for o in range(C * A - 1):
        summed = summed + owned_in[o]
    second_terms = unpack(summed, SPREAD, width_second, lax.rem(width_second * in_cxy, 128))
    unscaled = apply(system, second_terms / scale_column)

    norm = jnp.sum(unscaled * unscaled, axis=1, keepdims=True)
    norm_tile = jnp.zeros((8, 128), jnp.float32)
    for q in range(G):
        norm_tile = jnp.where(lane8 == q, group(norm, q), norm_tile)
    norms_xy[in_cxy] = norm_tile
    mine = norms_xy.at[in_cxy]
    send_all(mine, mine, 10, cxy_partner, C * A)
    arrived(norms_xy.at[pl.ds(0, C * A - 1)], 10)
    summed = norms_xy[0]
    for o in range(1, C * A):
        summed = summed + norms_xy[o]
    norms_z[b] = summed
    mine = norms_z.at[b]
    send_all(mine, mine, 11, z_partner, B)
    arrived(norms_z.at[pl.ds(0, B - 1)], 11)
    summed = norms_z[0]
    for o in range(1, B):
        summed = summed + norms_z[o]
    norm = stack([summed[:, q : q + 1] for q in range(G)])
    second_out[...] = (unscaled / jnp.sqrt(norm / K + EPSILON))[:, :width_second]

    left(second_slots.at[pl.ds(0, C * A - 1)], 0)
    left(first_slots.at[pl.ds(0, C * B - 1)], 1)
    left(terms_z.at[pl.ds(0, B - 1)], 2)
    left(grams_xy.at[pl.ds(0, A - 1)], 3)
    left(terms_xy.at[pl.ds(0, C * A - 1)], 4)
    left(half_in, 5)
    left(halves_z.at[pl.ds(0, B - 1)], 6)
    left(solved.at[0], 7)
    left(owned_in, 8)
    left(raw_xy.at[pl.ds(0, A - 1)], 9)
    left(norms_xy.at[pl.ds(0, C * A - 1)], 10)
    left(norms_z.at[pl.ds(0, B - 1)], 11)


def per_device(sizes, contacts, first_bins, second_bins):
    C, A, B, I, J, K = sizes
    cells, rows, columns = contacts.shape
    f32 = jnp.float32

    def tiles(*lead):
        return pltpu.VMEM(lead + (8, 128), f32)

    return tuple(
        pl.pallas_call(
            functools.partial(kernel, sizes),
            out_shape=(
                jax.ShapeDtypeStruct((R, cells), f32),
                jax.ShapeDtypeStruct(first_bins.shape, f32),
                jax.ShapeDtypeStruct(second_bins.shape, f32),
            ),
            in_specs=[pl.BlockSpec(memory_space=pl.ANY)] * 3,
            out_specs=[pl.BlockSpec(memory_space=pltpu.VMEM)] * 3,
            scratch_shapes=[
                pltpu.VMEM((cells, rows, columns), f32),
                pltpu.VMEM((cells * rows, columns), jnp.bfloat16),
                pltpu.VMEM((cells * rows, columns), jnp.bfloat16),
                pltpu.VMEM(first_bins.shape, f32),
                pltpu.VMEM(second_bins.shape, f32),
                pltpu.VMEM((R, 128), f32),
                pltpu.VMEM((R, 128), f32),
                tiles(C * B),
                tiles(C * A),
                tiles(B),
                tiles(A),
                tiles(C * A),
                pltpu.VMEM((cells // 2, R, 2 * rows), f32),
                pltpu.VMEM((2, R, 128), f32),
                pltpu.VMEM((R, 128), f32),
                pltpu.VMEM((B, R, 128), f32),
                pltpu.VMEM((2, R, 128), f32),
                tiles(A),
                tiles(C * A),
                tiles(C * A - 1),
                tiles(C * A),
                tiles(B),
                pltpu.SemaphoreType.DMA((2 + cells,)),
                pltpu.SemaphoreType.DMA((12,)),
                pltpu.SemaphoreType.DMA((12,)),
            ],
            compiler_params=pltpu.CompilerParams(
                collective_id=0, has_side_effects=True, vmem_limit_bytes=40 * 1024 * 1024
            ),
            name="sweep",
        )(contacts, first_bins, second_bins)
    )


def solution(mesh):
    placed = (
        P("cell", "bini", "binj"),
        P(None, ("bini", "cell", "binj")),
        P(None, ("binj", "cell", "bini")),
    )

    def whole(contacts, first_bins, second_bins):
        sizes = (
            mesh.shape["cell"],
            mesh.shape["bini"],
            mesh.shape["binj"],
            contacts.shape[0],
            first_bins.shape[1],
            second_bins.shape[1],
        )
        return jax.shard_map(
            functools.partial(per_device, sizes),
            mesh=mesh,
            in_specs=placed,
            out_specs=(
                P(None, "cell"),
                P(None, ("bini", "cell", "binj")),
                P(None, ("binj", "cell", "bini")),
            ),
            check_vma=False,
        )(contacts, first_bins, second_bins)

    return whole
```

```python
import functools

import jax
import jax.numpy as jnp
from jax import lax
from jax.experimental import pallas as pl
from jax.experimental.pallas import tpu as pltpu
from jax.sharding import PartitionSpec as P

EPSILON = 1e-06
PRECISE = lax.Precision.HIGHEST
MESH = pl.DeviceIdType.MESH
R = 24
G = 3
SPREAD = 40
NT = (((1,), (1,)), ((), ()))


def lanes(shape):
    return lax.broadcasted_iota(jnp.int32, shape, 1)


def group(value, q):
    return value[8 * q : 8 * q + 8, :]


def stack(tiles):
    return jnp.concatenate(tiles, axis=0)


def turn(value, shift):
    if isinstance(shift, int):
        shift = shift % 128
        return value if shift == 0 else pltpu.roll(value, shift, 1)
    return pltpu.roll(value, shift, 1)


def pack(value, step, base=None):
    out = None
    for q in range(G):
        if base is None:
            tile = turn(group(value, q), step * q)
        else:
            tile = turn(group(value, q), lax.rem(base + step * q, 128))
        out = tile if out is None else out + tile
    return out


def unpack(tile, step, width, base=None):
    parts = []
    for q in range(G):
        if base is None:
            part = turn(tile, -step * q)
        else:
            part = turn(tile, lax.rem(256 - base - step * q, 128))
        parts.append(jnp.where(lanes(part.shape) < width, part, 0.0))
    return stack(parts)


def within(lane, start, width):
    return ((lane - start) & 127) < width


def spread(tile_at, count, width, tiles):
    lane = lanes((8, 128))
    wholes = []
    for v in range(count // 2):
        wholes.extend(whole_pair(tile_at(v), SPREAD // 2))
    out = [[jnp.zeros((8, 128), jnp.float32) for _ in range(tiles)] for _ in range(G)]
    for o in range(count):
        tile = wholes[o]
        start = width * o
        for t in range(tiles):
            low, high = max(start, 128 * t), min(start + width, 128 * t + 128)
            if low >= high:
                continue
            for q in range(G):
                mask = within(lane, (low + SPREAD * q) % 128, high - low)
                out[q][t] = jnp.where(mask, tile, out[q][t])
    return [stack([turn(out[q][t], -SPREAD * q) for q in range(G)]) for t in range(tiles)]


def swap(tile):
    return pltpu.roll(tile, 4, 0)


def two(slots, v):
    return jnp.concatenate([slots[2 * v], slots[2 * v + 1]], axis=0)


def halve(tile, step):
    return (tile + turn(swap(tile), step))[:4]


def whole_pair(tile, step):
    upper = lax.broadcasted_iota(jnp.int32, (8, 128), 0) < 4
    swapped = swap(tile)
    return jnp.where(upper, tile, turn(swapped, -step)), jnp.where(upper, swapped, turn(tile, -step))


def flip(value):
    tall = jnp.concatenate([value, jnp.zeros((128 - R, 128), jnp.float32)], axis=0)
    return tall.T[:, :R]


def split(value):
    high = value.astype(jnp.bfloat16)
    return high, (value - high.astype(jnp.float32)).astype(jnp.bfloat16)


def split_rows(value):
    high = value.astype(jnp.bfloat16).astype(jnp.float32)
    return jnp.concatenate([high, value - high], axis=0).astype(jnp.bfloat16)


def gram(tiles):
    total = None
    for tile in tiles:
        tall = jnp.concatenate([tile, jnp.zeros((128 - R, 128), jnp.float32)], axis=0)
        part = lax.dot_general(tile, tall, NT, precision=PRECISE, preferred_element_type=jnp.float32)
        total = part if total is None else total + part
    return total


def inverse(a):
    lane, row = lanes((R, 128)), lax.broadcasted_iota(jnp.int32, (R, 128), 0)
    for k in range(R):
        pivot_row = a[k : k + 1, :]
        pivot_column = a[:, k : k + 1]
        over = 1.0 / a[k : k + 1, k : k + 1]
        new_row = jnp.where(lane[:1] == k, over, pivot_row * over)
        a = jnp.where(lane == k, 0.0, a) - pivot_column * new_row
        a = jnp.where(row == k, new_row, a)
    return a


def apply(matrix, value):
    total = None
    for s in range(R):
        term = matrix[:, s : s + 1] * value[s : s + 1, :]
        total = term if total is None else total + term
    return total


def diagonal_scales(raw, count):
    lane, row = lanes((R, 128)), lax.broadcasted_iota(jnp.int32, (R, 128), 0)
    diagonal = jnp.where(lane == row, raw, 0.0)
    column = jnp.sum(diagonal, axis=1, keepdims=True)
    across = jnp.sum(diagonal, axis=0, keepdims=True)
    return jnp.sqrt(column / count + EPSILON), jnp.sqrt(across / count + EPSILON)


def kernel(
    sizes,
    contacts,
    first_in,
    second_in,
    out,
    x_full,
    x_high,
    x_low,
    first_land,
    second_land,
    pad,
    first_slots,
    second_slots,
    terms_z,
    grams_xy,
    terms_xy,
    products,
    halves,
    half_in,
    halves_z,
    solved,
    raw_xy,
    parts,
    part_in,
    parts_xy,
    norms,
    load_sem,
    send_sem,
    recv_sem,
):
    C, A, B, I, J, K = sizes
    cells, rows = x_full.shape[0], x_full.shape[1]
    width_first, width_second = rows // (C * B), x_full.shape[2] // (C * A)
    c, a, b = lax.axis_index("cell"), lax.axis_index("bini"), lax.axis_index("binj")
    in_cz, in_cxy = c * B + b, c * A + a
    other = (1 - c, a, b)
    lane8, lane24 = lanes((8, 128)), lanes((R, 128))
    upper8 = lax.broadcasted_iota(jnp.int32, (8, 128), 0) < 4

    loads = [
        pltpu.make_async_copy(second_in, second_land, load_sem.at[0]),
        pltpu.make_async_copy(first_in, first_land, load_sem.at[1]),
    ]
    for load in loads:
        load.start()

    def load_cell(i):
        return pltpu.make_async_copy(contacts.at[i], x_full.at[i], load_sem.at[2 + i])

    for i in range(cells):
        load_cell(i).start()

    barrier = pltpu.get_barrier_semaphore()

    def signal(device):
        pl.semaphore_signal(barrier, inc=1, device_id=device, device_id_type=MESH)

    def z_partner(k):
        return (c, a, lax.rem(b + k, B))

    def xy_partner(k):
        return (c, lax.rem(a + k, A), b)

    def cz_partner(k):
        return (lax.rem(c + k // B, C), a, lax.rem(b + lax.rem(k, B), B))

    def cxy_partner(k):
        return (lax.rem(c + k // A, C), lax.rem(a + lax.rem(k, A), A), b)

    def greet_cz(k, carry):
        signal(cz_partner(k))
        return carry

    def greet_cxy(k, carry):
        signal(cxy_partner(k))
        return carry

    lax.fori_loop(1, C * B, greet_cz, 0)
    lax.fori_loop(1, A, greet_cxy, 0)
    lax.fori_loop(A + 1, C * A, greet_cxy, 0)

    pad[...] = jnp.zeros_like(pad)
    loads[0].wait()
    pad[:width_second, :R] = second_land[...]
    packed = pack(pad[...].T[:R], SPREAD, lax.rem(width_second * in_cxy, 128))
    second_slots[in_cxy] = halve(packed, SPREAD // 2)
    loads[1].wait()
    pad[:width_first, :R] = first_land[...]
    packed = pack(pad[...].T[:R], SPREAD, lax.rem(width_first * in_cz, 128))
    first_slots[in_cz] = halve(packed, SPREAD // 2)

    def send(source, target, number, device):
        pltpu.make_async_remote_copy(
            source, target, send_sem.at[number], recv_sem.at[number], device_id=device, device_id_type=MESH
        ).start()

    def send_all(source, target, number, partner, count):
        def one(k, carry):
            send(source, target, number, partner(k))
            return carry

        lax.fori_loop(1, count, one, 0)

    def arrived(like, number):
        pltpu.make_async_copy(like, like, recv_sem.at[number]).wait()

    def left(like, number):
        pltpu.make_async_copy(like, like, send_sem.at[number]).wait()

    def split_cell(i, carry):
        load_cell(i).wait()
        high, low = split(x_full[i])
        at = pl.ds(pl.multiple_of(i * rows, rows), rows)
        x_high[at, :] = high
        x_low[at, :] = low
        return carry

    lax.fori_loop(0, cells // 2, split_cell, 0)
    pl.semaphore_wait(barrier, C * B - 1 + C * (A - 1))

    mine = second_slots.at[in_cxy]
    send_all(mine, mine, 0, cxy_partner, C * A)
    mine = first_slots.at[in_cz]
    send_all(mine, mine, 1, cz_partner, C * B)
    lax.fori_loop(cells // 2, cells, split_cell, 0)

    arrived(second_slots.at[pl.ds(0, C * A - 1)], 0)
    second = spread(lambda v: two(second_slots, v), C * A, width_second, 3)
    second_rows = split_rows(jnp.concatenate(second, axis=1))
    arrived(first_slots.at[pl.ds(0, C * B - 1)], 1)
    first = spread(lambda v: two(first_slots, v), C * B, width_first, 2)
    first_turned = [turn(group(first[0], q), 64) for q in range(G)]
    first_turned = stack(first_turned)
    last_turned = stack([turn(group(first[1], q), 64) for q in range(G)])
    first_pair = [
        first[0],
        jnp.where(lane24 < 64, first[1], first_turned),
        jnp.where(lane24 < 64, first_turned, last_turned),
    ]

    cell_terms = jnp.zeros((R, 128), jnp.float32)
    for p in range(cells // 2):
        at = pl.ds(2 * rows * p, 2 * rows)
        big = lax.dot_general(second_rows, x_high[at, :], NT, preferred_element_type=jnp.float32)
        small = lax.dot_general(second_rows, x_low[at, :], NT, preferred_element_type=jnp.float32)
        both = (small[:R] + small[R:]) + big[R:] + big[:R]
        products[p] = both
        terms = [both[:, 128 * t : 128 * t + 128] * first_pair[t] for t in range(3)]
        even = jnp.sum(terms[0] + jnp.where(lane24 < 64, terms[1], 0.0), axis=1, keepdims=True)
        odd = jnp.sum(terms[2] + jnp.where(lane24 < 64, 0.0, terms[1]), axis=1, keepdims=True)
        cell_terms = jnp.where(lane24 == 2 * p, even, cell_terms)
        cell_terms = jnp.where(lane24 == 2 * p + 1, odd, cell_terms)

    terms_z[b] = pack(cell_terms, cells) + turn(pack(gram(second), R), 56)
    mine = terms_z.at[b]
    send_all(mine, mine, 2, z_partner, B)
    grams_xy[a] = pack(gram(first), R)
    mine = grams_xy.at[a]
    send_all(mine, mine, 3, xy_partner, A)

    arrived(terms_z.at[pl.ds(0, B - 1)], 2)
    summed = terms_z[0]
    for o in range(1, B):
        summed = summed + terms_z[o]
    terms_xy[in_cxy] = halve(jnp.where(lane8 < G * cells, summed, 0.0), G * cells)
    mine = terms_xy.at[in_cxy]
    send_all(mine, mine, 4, cxy_partner, C * A)

    gram_second = unpack(turn(summed, -56), R, R)
    arrived(grams_xy.at[pl.ds(0, A - 1)], 3)
    summed = grams_xy[0]
    for o in range(1, A):
        summed = summed + grams_xy[o]
    gram_first = unpack(summed, R, R)
    system = inverse(gram_first * gram_second)

    arrived(terms_xy.at[pl.ds(0, C * A - 1)], 4)
    cell_total = None
    for core in range(C):
        summed = terms_xy[core * A]
        for o in range(1, A):
            summed = summed + terms_xy[core * A + o]
        summed = jnp.concatenate([summed, summed], axis=0)
        block = unpack(jnp.where(upper8, summed, turn(summed, -G * cells)), cells, cells)
        block = stack([turn(group(block, q), cells * core) for q in range(G)])
        cell_total = block if cell_total is None else cell_total + block

    unscaled = apply(system, cell_total)
    scale = jnp.sqrt(jnp.sum(unscaled * unscaled, axis=1, keepdims=True) / I + EPSILON)
    cell_factor = unscaled / scale
    own_cells = stack([turn(group(cell_factor, q), lax.rem(128 - cells * c, 128)) for q in range(G)])

    pair_sum = [jnp.zeros((R, 128), jnp.float32) for _ in range(3)]
    weights = []
    for p in range(cells // 2):
        even = jnp.broadcast_to(own_cells[:, 2 * p : 2 * p + 1], (R, 128))
        odd = jnp.broadcast_to(own_cells[:, 2 * p + 1 : 2 * p + 2], (R, 128))
        weight = [even, jnp.where(lane24 < 64, even, odd), odd]
        weights.append(weight)
        both = products[p]
        for t in range(3):
            pair_sum[t] = pair_sum[t] + both[:, 128 * t : 128 * t + 128] * weight[t]

    def half_turn(value):
        return stack([turn(group(value, q), 64) for q in range(G)])

    turned = [half_turn(pair_sum[1]), half_turn(pair_sum[2])]
    halves[0] = pair_sum[0] + jnp.where(lane24 < 64, turned[0], turned[1])
    halves[1] = jnp.where(lane24 < 64, pair_sum[1] + turned[1], 0.0)
    send(halves.at[1 - c], half_in, 5, other)

    raw = gram([unscaled])
    scale_column, scale_row = diagonal_scales(raw, I)
    gram_cells = jnp.where(lane24 < R, raw / (scale_column * scale_row), 0.0)
    out[:cells, :] = flip(own_cells)[:cells]

    arrived(half_in, 5)
    halves_z[b] = halves[c] + half_in[...]
    mine = halves_z.at[b]
    send_all(mine, mine, 6, z_partner, B)
    system = inverse(gram_cells * gram_second)
    arrived(halves_z.at[pl.ds(0, B - 1)], 6)
    summed = halves_z[0]
    for o in range(1, B):
        summed = summed + halves_z[o]
    solved[c] = apply(system, summed)
    mine = solved.at[c]
    send(mine, mine, 7, other)
    arrived(solved.at[0], 7)
    low, high = solved[0], solved[1]

    low_turned, high_turned = half_turn(low), half_turn(high)
    solved_pair = [
        low,
        jnp.where(lane24 < 64, high, low_turned),
        jnp.where(lane24 < 64, low_turned, high_turned),
    ]
    total = None
    for p in range(cells // 2):
        at = pl.ds(2 * rows * p, 2 * rows)
        left_rows = split_rows(
            jnp.concatenate([solved_pair[t] * weights[p][t] for t in range(3)], axis=1)
        )
        big = jnp.dot(left_rows, x_high[at, :], preferred_element_type=jnp.float32)
        small = jnp.dot(left_rows, x_low[at, :], preferred_element_type=jnp.float32)
        both = big + small
        total = both if total is None else total + both
    total = total[:R] + total[R:]

    tiles = [total[:, 128 * t : 128 * t + 128] for t in range(3)]
    middle = half_turn(tiles[1])
    joined = half_turn(tiles[2])
    blocks = (
        (tiles[0], jnp.where(lane24 < 64, tiles[1], 0.0)),
        (jnp.where(lane24 < 64, middle, joined), jnp.where(lane24 < 64, joined, 0.0)),
    )
    for core in range(2):
        low, high = blocks[core]
        parts[core, :R] = low
        parts[core, R : R + 8] = group(high, 0) + turn(group(high, 1), 64)
        parts[core, R + 8 :] = group(high, 2)
    send(parts.at[1 - c], part_in, 8, other)

    raw_xy[a] = pack(gram([solved[0], solved[1]]), R)
    mine = raw_xy.at[a]
    send_all(mine, mine, 9, xy_partner, A)
    arrived(part_in, 8)
    parts_xy[a] = parts[c] + part_in[...]
    mine = parts_xy.at[a]
    send_all(mine, mine, 10, xy_partner, A)

    arrived(raw_xy.at[pl.ds(0, A - 1)], 9)
    summed = raw_xy[0]
    for o in range(1, A):
        summed = summed + raw_xy[o]
    raw = unpack(summed, R, R)
    scale_column, scale_row = diagonal_scales(raw, J)
    gram_first = jnp.where(lane24 < R, raw / (scale_column * scale_row), 0.0)
    system = inverse(gram_cells * gram_first) / scale_row
    start = width_first * in_cz
    at_low = lax.rem(256 - start, 128)
    piece = [
        jnp.where(lane8 < 128 - start, turn(group(solved[0], q), at_low), turn(group(solved[1], q), at_low))
        for q in range(G)
    ]
    out[cells : cells + width_first, :] = flip(stack(piece) / scale_column)[:width_first]

    arrived(parts_xy.at[pl.ds(0, A - 1)], 10)
    summed = parts_xy[0]
    for o in range(1, A):
        summed = summed + parts_xy[o]
    mixed = summed[R : R + 8]
    low = summed[:R]
    high = [jnp.where(lane8 < 64, mixed, 0.0), jnp.where(lane8 < 64, turn(mixed, 64), 0.0), summed[R + 8 :]]
    low, high = apply(system, low), apply(system, stack(high))

    norm = jnp.sum(low * low + high * high, axis=1, keepdims=True)
    row24 = lax.broadcasted_iota(jnp.int32, (R, 128), 0)
    norms[in_cz] = jnp.sum(jnp.where(lane24 == row24, norm, 0.0), axis=0, keepdims=True)
    mine = norms.at[in_cz]
    send_all(mine, mine, 11, cz_partner, C * B)
    start = width_second * a
    at_low = lax.rem(256 - start, 128)
    piece = [
        jnp.where(lane8 < 128 - start, turn(group(low, q), at_low), turn(group(high, q), at_low))
        for q in range(G)
    ]
    piece = flip(stack(piece))[:width_second]
    arrived(norms.at[pl.ds(0, C * B - 1)], 11)
    norm = norms[0]
    for o in range(1, C * B):
        norm = norm + norms[o]
    out[cells + 16 : cells + 16 + width_second, :] = piece / jnp.sqrt(norm / K + EPSILON)[:, :R]

    left(second_slots.at[pl.ds(0, C * A - 1)], 0)
    left(first_slots.at[pl.ds(0, C * B - 1)], 1)
    left(terms_z.at[pl.ds(0, B - 1)], 2)
    left(grams_xy.at[pl.ds(0, A - 1)], 3)
    left(terms_xy.at[pl.ds(0, C * A - 1)], 4)
    left(half_in, 5)
    left(halves_z.at[pl.ds(0, B - 1)], 6)
    left(solved.at[0], 7)
    left(part_in, 8)
    left(raw_xy.at[pl.ds(0, A - 1)], 9)
    left(parts_xy.at[pl.ds(0, A - 1)], 10)
    left(norms.at[pl.ds(0, C * B - 1)], 11)


def share(counts, out, cells, first, second, sem):
    copies = [
        pltpu.make_async_copy(out.at[pl.ds(16 * n, counts[n])], target, sem.at[n])
        for n, target in enumerate((cells, first, second))
    ]
    for copy in copies:
        copy.start()
    for copy in copies:
        copy.wait()


def per_device(sizes, contacts, first_bins, second_bins):
    C, A, B, I, J, K = sizes
    cells, rows, columns = contacts.shape
    f32 = jnp.float32

    def tiles(*lead):
        return pltpu.VMEM(lead + (8, 128), f32)

    first_bins, second_bins = first_bins.T, second_bins.T
    out = (
        pl.pallas_call(
            functools.partial(kernel, sizes),
            out_shape=jax.ShapeDtypeStruct((cells + 32, R), f32),
            in_specs=[pl.BlockSpec(memory_space=pl.ANY)] * 3,
            out_specs=pl.BlockSpec(memory_space=pltpu.VMEM),
            scratch_shapes=[
                pltpu.VMEM((cells, rows, columns), f32),
                pltpu.VMEM((cells * rows, columns), jnp.bfloat16),
                pltpu.VMEM((cells * rows, columns), jnp.bfloat16),
                pltpu.VMEM(first_bins.shape, f32),
                pltpu.VMEM(second_bins.shape, f32),
                pltpu.VMEM((128, 128), f32),
                pltpu.VMEM((C * B, 4, 128), f32),
                pltpu.VMEM((C * A, 4, 128), f32),
                tiles(B),
                tiles(A),
                pltpu.VMEM((C * A, 4, 128), f32),
                pltpu.VMEM((cells // 2, R, 2 * rows), f32),
                pltpu.VMEM((2, R, 128), f32),
                pltpu.VMEM((R, 128), f32),
                pltpu.VMEM((B, R, 128), f32),
                pltpu.VMEM((2, R, 128), f32),
                tiles(A),
                pltpu.VMEM((2, R + 16, 128), f32),
                pltpu.VMEM((R + 16, 128), f32),
                pltpu.VMEM((A, R + 16, 128), f32),
                pltpu.VMEM((C * B, 1, 128), f32),
                pltpu.SemaphoreType.DMA((2 + cells,)),
                pltpu.SemaphoreType.DMA((12,)),
                pltpu.SemaphoreType.DMA((12,)),
            ],
            compiler_params=pltpu.CompilerParams(
                collective_id=0, has_side_effects=True, vmem_limit_bytes=60 * 1024 * 1024
            ),
            name="sweep",
        )(contacts, first_bins, second_bins)
    )
    counts = (cells, first_bins.shape[0], second_bins.shape[0])
    shares = pl.pallas_call(
        functools.partial(share, counts),
        out_shape=tuple(jax.ShapeDtypeStruct((n, R), f32) for n in counts),
        in_specs=[pl.BlockSpec(memory_space=pl.ANY)],
        out_specs=[pl.BlockSpec(memory_space=pl.ANY)] * 3,
        scratch_shapes=[pltpu.SemaphoreType.DMA((3,))],
        name="share",
    )(out)
    return tuple(piece.T for piece in shares)


def solution(mesh):
    placed = (
        P("cell", "bini", "binj"),
        P(None, ("bini", "cell", "binj")),
        P(None, ("binj", "cell", "bini")),
    )

    def whole(contacts, first_bins, second_bins):
        sizes = (
            mesh.shape["cell"],
            mesh.shape["bini"],
            mesh.shape["binj"],
            contacts.shape[0],
            first_bins.shape[1],
            second_bins.shape[1],
        )
        return jax.shard_map(
            functools.partial(per_device, sizes),
            mesh=mesh,
            in_specs=placed,
            out_specs=(
                P(None, "cell"),
                P(None, ("bini", "cell", "binj")),
                P(None, ("binj", "cell", "bini")),
            ),
            check_vma=False,
        )(contacts, first_bins, second_bins)

    return whole
```

```python
import functools

import jax
import jax.numpy as jnp
from jax import lax
from jax.experimental import pallas as pl
from jax.experimental.pallas import tpu as pltpu
from jax.sharding import PartitionSpec as P

EPSILON = 1e-06
PRECISE = lax.Precision.HIGHEST
MESH = pl.DeviceIdType.MESH
R = 24
G = 3
SPREAD = 40
NT = (((1,), (1,)), ((), ()))


def lanes(shape):
    return lax.broadcasted_iota(jnp.int32, shape, 1)


def group(value, q):
    return value[8 * q : 8 * q + 8, :]


def stack(tiles):
    return jnp.concatenate(tiles, axis=0)


def turn(value, shift):
    if isinstance(shift, int):
        shift = shift % 128
        return value if shift == 0 else pltpu.roll(value, shift, 1)
    return pltpu.roll(value, shift, 1)


def pack(value, step, base=None):
    out = None
    for q in range(G):
        if base is None:
            tile = turn(group(value, q), step * q)
        else:
            tile = turn(group(value, q), lax.rem(base + step * q, 128))
        out = tile if out is None else out + tile
    return out


def unpack(tile, step, width, base=None):
    parts = []
    for q in range(G):
        if base is None:
            part = turn(tile, -step * q)
        else:
            part = turn(tile, lax.rem(256 - base - step * q, 128))
        parts.append(jnp.where(lanes(part.shape) < width, part, 0.0))
    return stack(parts)


def within(lane, start, width):
    return ((lane - start) & 127) < width


def spread(tile_at, count, width, tiles):
    lane = lanes((8, 128))
    wholes = []
    for v in range(count // 2):
        wholes.extend(whole_pair(tile_at(v), SPREAD // 2))
    out = [[jnp.zeros((8, 128), jnp.float32) for _ in range(tiles)] for _ in range(G)]
    for o in range(count):
        tile = wholes[o]
        start = width * o
        for t in range(tiles):
            low, high = max(start, 128 * t), min(start + width, 128 * t + 128)
            if low >= high:
                continue
            for q in range(G):
                mask = within(lane, (low + SPREAD * q) % 128, high - low)
                out[q][t] = jnp.where(mask, tile, out[q][t])
    return [stack([turn(out[q][t], -SPREAD * q) for q in range(G)]) for t in range(tiles)]


def swap(tile):
    return pltpu.roll(tile, 4, 0)


def two(slots, v):
    return jnp.concatenate([slots[2 * v], slots[2 * v + 1]], axis=0)


def halve(tile, step):
    return (tile + turn(swap(tile), step))[:4]


def whole_pair(tile, step):
    upper = lax.broadcasted_iota(jnp.int32, (8, 128), 0) < 4
    swapped = swap(tile)
    return jnp.where(upper, tile, turn(swapped, -step)), jnp.where(upper, swapped, turn(tile, -step))


def flip(value):
    tall = jnp.concatenate([value, jnp.zeros((128 - R, 128), jnp.float32)], axis=0)
    return tall.T[:, :R]


def split(value):
    high = value.astype(jnp.bfloat16)
    return high, (value - high.astype(jnp.float32)).astype(jnp.bfloat16)


def split_rows(value):
    high = value.astype(jnp.bfloat16).astype(jnp.float32)
    return jnp.concatenate([high, value - high], axis=0).astype(jnp.bfloat16)


def gram(tiles):
    total = None
    for tile in tiles:
        tall = jnp.concatenate([tile, jnp.zeros((128 - R, 128), jnp.float32)], axis=0)
        part = lax.dot_general(tile, tall, NT, precision=PRECISE, preferred_element_type=jnp.float32)
        total = part if total is None else total + part
    return total


def inverse(a):
    lane, row = lanes((R, 128)), lax.broadcasted_iota(jnp.int32, (R, 128), 0)
    for k in range(R):
        pivot_row = a[k : k + 1, :]
        pivot_column = a[:, k : k + 1]
        over = 1.0 / a[k : k + 1, k : k + 1]
        new_row = jnp.where(lane[:1] == k, over, pivot_row * over)
        a = jnp.where(lane == k, 0.0, a) - pivot_column * new_row
        a = jnp.where(row == k, new_row, a)
    return a


def widen(matrix, wide):
    for s in range(R):
        wide[s] = jnp.broadcast_to(matrix[:, s : s + 1], (R, 128))


def apply(wide, value):
    total = None
    for s in range(R):
        term = wide[s] * value[s : s + 1, :]
        total = term if total is None else total + term
    return total


def diagonal_scales(raw, count):
    lane, row = lanes((R, 128)), lax.broadcasted_iota(jnp.int32, (R, 128), 0)
    diagonal = jnp.where(lane == row, raw, 0.0)
    column = jnp.sum(diagonal, axis=1, keepdims=True)
    across = jnp.sum(diagonal, axis=0, keepdims=True)
    return jnp.sqrt(column / count + EPSILON), jnp.sqrt(across / count + EPSILON)


def kernel(
    sizes,
    contacts,
    first_in,
    second_in,
    out,
    x_full,
    x_parts,
    x_turned,
    first_land,
    second_land,
    pad,
    first_slots,
    second_slots,
    terms_z,
    grams_xy,
    terms_xy,
    products,
    halves,
    half_in,
    halves_z,
    solved,
    raw_xy,
    parts,
    part_in,
    parts_xy,
    norms,
    wide_system,
    load_sem,
    send_sem,
    recv_sem,
):
    C, A, B, I, J, K = sizes
    cells, rows, columns = x_full.shape
    width_first, width_second = rows // (C * B), x_full.shape[2] // (C * A)
    c, a, b = lax.axis_index("cell"), lax.axis_index("bini"), lax.axis_index("binj")
    in_cz, in_cxy = c * B + b, c * A + a
    other = (1 - c, a, b)
    lane8, lane24 = lanes((8, 128)), lanes((R, 128))
    upper8 = lax.broadcasted_iota(jnp.int32, (8, 128), 0) < 4

    barrier = pltpu.get_barrier_semaphore()

    def signal(device):
        pl.semaphore_signal(barrier, inc=1, device_id=device, device_id_type=MESH)

    def flipped(m, size):
        first = size // 2 if size == B else size // 2 + size // 8
        m = m + first
        return jnp.where(m >= size, m - size + 1, m)

    def z_partner(m):
        return (c, a, b ^ flipped(m, B))

    def xy_partner(m):
        return (c, a ^ flipped(m, A), b)

    def across(device):
        return (1 - c, device[1], device[2])

    def over(count, partner, both, action):
        def one(m, carry):
            device = partner(m)
            action(device)
            if both:
                action(across(device))
            return carry

        lax.fori_loop(0, count - 1, one, 0)
        if both:
            action(other)

    z_partners, cz_partners = (B, z_partner, False), (B, z_partner, True)
    xy_partners, cxy_partners = (A, xy_partner, False), (A, xy_partner, True)
    over(*cxy_partners, signal)
    over(B, z_partner, False, signal)
    over(B, lambda m: across(z_partner(m)), False, signal)

    loads = [
        pltpu.make_async_copy(second_in, second_land, load_sem.at[0]),
        pltpu.make_async_copy(first_in, first_land, load_sem.at[1]),
    ]
    for load in loads:
        load.start()

    def load_cell(i):
        return pltpu.make_async_copy(contacts.at[i], x_full.at[i], load_sem.at[2 + i])

    for i in range(cells):
        load_cell(i).start()

    pad[...] = jnp.zeros_like(pad)
    loads[0].wait()
    pad[:width_second, :R] = second_land[...]
    packed = pack(pad[...].T[:R], SPREAD, lax.rem(width_second * in_cxy, 128))
    second_slots[in_cxy] = halve(packed, SPREAD // 2)
    loads[1].wait()
    pad[:width_first, :R] = first_land[...]
    packed = pack(pad[...].T[:R], SPREAD, lax.rem(width_first * in_cz, 128))
    first_slots[in_cz] = halve(packed, SPREAD // 2)

    def send(source, target, number, device):
        pltpu.make_async_remote_copy(
            source, target, send_sem.at[number], recv_sem.at[number], device_id=device, device_id_type=MESH
        ).start()

    def send_all(source, target, number, partners):
        over(*partners, lambda device: send(source, target, number, device))

    def arrived(like, number):
        pltpu.make_async_copy(like, like, recv_sem.at[number]).wait()

    def left(like, number):
        pltpu.make_async_copy(like, like, send_sem.at[number]).wait()

    def split_pair(p, carry):
        load_cell(2 * p).wait()
        load_cell(2 * p + 1).wait()
        pair = x_full[pl.ds(2 * p, 2)].reshape(2 * rows, columns)
        at = pl.ds(pl.multiple_of(2 * rows * p, 2 * rows), 2 * rows)
        x_parts[at, :columns], x_parts[at, columns:] = split(pair)
        x_turned[:columns, at], x_turned[columns:, at] = split(pair.T)
        return carry

    pl.semaphore_wait(barrier, C * B - 1 + C * (A - 1))

    mine = second_slots.at[in_cxy]
    send_all(mine, mine, 0, cxy_partners)
    mine = first_slots.at[in_cz]
    send_all(mine, mine, 1, cz_partners)
    lax.fori_loop(0, cells // 2, split_pair, 0)

    arrived(second_slots.at[pl.ds(0, C * A - 1)], 0)
    second = spread(lambda v: two(second_slots, v), C * A, width_second, 3)
    second_rows = split_rows(jnp.concatenate(second, axis=1))
    second_rows = jnp.concatenate([second_rows, second_rows], axis=1)
    arrived(first_slots.at[pl.ds(0, C * B - 1)], 1)
    first = spread(lambda v: two(first_slots, v), C * B, width_first, 2)
    first_turned = [turn(group(first[0], q), 64) for q in range(G)]
    first_turned = stack(first_turned)
    last_turned = stack([turn(group(first[1], q), 64) for q in range(G)])
    first_pair = [
        first[0],
        jnp.where(lane24 < 64, first[1], first_turned),
        jnp.where(lane24 < 64, first_turned, last_turned),
    ]

    cell_terms = jnp.zeros((R, 128), jnp.float32)
    for p in range(cells // 2):
        if p % 2 == 0:
            at = pl.ds(2 * rows * p, 4 * rows)
            wide = jnp.dot(second_rows, x_turned[:, at], preferred_element_type=jnp.float32)
            wide = wide[:R] + wide[R:]
        both = wide[:, 2 * rows * (p % 2) : 2 * rows * (p % 2 + 1)]
        products[p] = both
        terms = [both[:, 128 * t : 128 * t + 128] * first_pair[t] for t in range(3)]
        even = jnp.sum(terms[0] + jnp.where(lane24 < 64, terms[1], 0.0), axis=1, keepdims=True)
        odd = jnp.sum(terms[2] + jnp.where(lane24 < 64, 0.0, terms[1]), axis=1, keepdims=True)
        cell_terms = jnp.where(lane24 == 2 * p, even, cell_terms)
        cell_terms = jnp.where(lane24 == 2 * p + 1, odd, cell_terms)

    terms_z[b] = pack(cell_terms, cells) + turn(pack(gram(second), R), 56)
    mine = terms_z.at[b]
    send_all(mine, mine, 2, z_partners)
    grams_xy[a] = pack(gram(first), R)
    mine = grams_xy.at[a]
    send_all(mine, mine, 3, xy_partners)

    arrived(terms_z.at[pl.ds(0, B - 1)], 2)
    summed = terms_z[0]
    for o in range(1, B):
        summed = summed + terms_z[o]
    terms_xy[in_cxy] = halve(jnp.where(lane8 < G * cells, summed, 0.0), G * cells)
    mine = terms_xy.at[in_cxy]
    send_all(mine, mine, 4, cxy_partners)

    gram_second = unpack(turn(summed, -56), R, R)
    arrived(grams_xy.at[pl.ds(0, A - 1)], 3)
    summed = grams_xy[0]
    for o in range(1, A):
        summed = summed + grams_xy[o]
    gram_first = unpack(summed, R, R)
    widen(inverse(gram_first * gram_second), wide_system)

    arrived(terms_xy.at[pl.ds(0, C * A - 1)], 4)
    cell_total = None
    for core in range(C):
        summed = terms_xy[core * A]
        for o in range(1, A):
            summed = summed + terms_xy[core * A + o]
        summed = jnp.concatenate([summed, summed], axis=0)
        block = unpack(jnp.where(upper8, summed, turn(summed, -G * cells)), cells, cells)
        block = stack([turn(group(block, q), cells * core) for q in range(G)])
        cell_total = block if cell_total is None else cell_total + block

    unscaled = apply(wide_system, cell_total)
    scale = jnp.sqrt(jnp.sum(unscaled * unscaled, axis=1, keepdims=True) / I + EPSILON)
    cell_factor = unscaled / scale
    own_cells = stack([turn(group(cell_factor, q), lax.rem(128 - cells * c, 128)) for q in range(G)])

    pair_sum = [jnp.zeros((R, 128), jnp.float32) for _ in range(3)]
    weights = []
    for p in range(cells // 2):
        even = jnp.broadcast_to(own_cells[:, 2 * p : 2 * p + 1], (R, 128))
        odd = jnp.broadcast_to(own_cells[:, 2 * p + 1 : 2 * p + 2], (R, 128))
        weight = [even, jnp.where(lane24 < 64, even, odd), odd]
        weights.append(weight)
        both = products[p]
        for t in range(3):
            pair_sum[t] = pair_sum[t] + both[:, 128 * t : 128 * t + 128] * weight[t]

    def half_turn(value):
        return stack([turn(group(value, q), 64) for q in range(G)])

    turned = [half_turn(pair_sum[1]), half_turn(pair_sum[2])]
    halves[0] = pair_sum[0] + jnp.where(lane24 < 64, turned[0], turned[1])
    halves[1] = jnp.where(lane24 < 64, pair_sum[1] + turned[1], 0.0)
    send(halves.at[1 - c], half_in, 5, other)

    arrived(half_in, 5)
    halves_z[b] = halves[c] + half_in[...]
    mine = halves_z.at[b]
    send_all(mine, mine, 6, z_partners)
    raw = gram([unscaled])
    scale_column, scale_row = diagonal_scales(raw, I)
    gram_cells = jnp.where(lane24 < R, raw / (scale_column * scale_row), 0.0)
    out[:cells, :] = flip(own_cells)[:cells]
    widen(inverse(gram_cells * gram_second), wide_system)
    arrived(halves_z.at[pl.ds(0, B - 1)], 6)
    summed = halves_z[0]
    for o in range(1, B):
        summed = summed + halves_z[o]
    solved[c] = apply(wide_system, summed)
    mine = solved.at[c]
    send(mine, mine, 7, other)
    arrived(solved.at[0], 7)
    low, high = solved[0], solved[1]

    low_turned, high_turned = half_turn(low), half_turn(high)
    solved_pair = [
        low,
        jnp.where(lane24 < 64, high, low_turned),
        jnp.where(lane24 < 64, low_turned, high_turned),
    ]
    total = None
    for p in range(0, cells // 2, 2):
        left_rows = split_rows(
            jnp.concatenate([solved_pair[t] * weights[p + h][t] for h in range(2) for t in range(3)], axis=1)
        )
        both = jnp.dot(left_rows, x_parts[pl.ds(2 * rows * p, 4 * rows), :], preferred_element_type=jnp.float32)
        total = both if total is None else total + both
    total = total[:, :columns] + total[:, columns:]
    total = total[:R] + total[R:]

    tiles = [total[:, 128 * t : 128 * t + 128] for t in range(3)]
    middle = half_turn(tiles[1])
    joined = half_turn(tiles[2])
    blocks = (
        (tiles[0], jnp.where(lane24 < 64, tiles[1], 0.0)),
        (jnp.where(lane24 < 64, middle, joined), jnp.where(lane24 < 64, joined, 0.0)),
    )
    for core in range(2):
        low, high = blocks[core]
        parts[core, :R] = low
        parts[core, R : R + 8] = group(high, 0) + turn(group(high, 1), 64)
        parts[core, R + 8 :] = group(high, 2)
    send(parts.at[1 - c], part_in, 8, other)

    raw_xy[a] = pack(gram([solved[0], solved[1]]), R)
    mine = raw_xy.at[a]
    send_all(mine, mine, 9, xy_partners)
    arrived(part_in, 8)
    parts_xy[a] = parts[c] + part_in[...]
    mine = parts_xy.at[a]
    send_all(mine, mine, 10, xy_partners)

    arrived(raw_xy.at[pl.ds(0, A - 1)], 9)
    summed = raw_xy[0]
    for o in range(1, A):
        summed = summed + raw_xy[o]
    raw = unpack(summed, R, R)
    scale_column, scale_row = diagonal_scales(raw, J)
    gram_first = jnp.where(lane24 < R, raw / (scale_column * scale_row), 0.0)
    widen(inverse(gram_cells * gram_first) / scale_row, wide_system)
    start = width_first * in_cz
    at_low = lax.rem(256 - start, 128)
    piece = [
        jnp.where(lane8 < 128 - start, turn(group(solved[0], q), at_low), turn(group(solved[1], q), at_low))
        for q in range(G)
    ]
    out[cells : cells + width_first, :] = flip(stack(piece) / scale_column)[:width_first]

    arrived(parts_xy.at[pl.ds(0, A - 1)], 10)
    summed = parts_xy[0]
    for o in range(1, A):
        summed = summed + parts_xy[o]
    mixed = summed[R : R + 8]
    low = summed[:R]
    high = [jnp.where(lane8 < 64, mixed, 0.0), jnp.where(lane8 < 64, turn(mixed, 64), 0.0), summed[R + 8 :]]
    low, high = apply(wide_system, low), apply(wide_system, stack(high))

    norm = jnp.sum(low * low + high * high, axis=1, keepdims=True)
    row24 = lax.broadcasted_iota(jnp.int32, (R, 128), 0)
    norms[in_cz] = jnp.sum(jnp.where(lane24 == row24, norm, 0.0), axis=0, keepdims=True)
    mine = norms.at[in_cz]
    send_all(mine, mine, 11, cz_partners)
    start = width_second * a
    at_low = lax.rem(256 - start, 128)
    piece = [
        jnp.where(lane8 < 128 - start, turn(group(low, q), at_low), turn(group(high, q), at_low))
        for q in range(G)
    ]
    piece = flip(stack(piece))[:width_second]
    arrived(norms.at[pl.ds(0, C * B - 1)], 11)
    norm = norms[0]
    for o in range(1, C * B):
        norm = norm + norms[o]
    out[cells + 16 : cells + 16 + width_second, :] = piece / jnp.sqrt(norm / K + EPSILON)[:, :R]

    left(second_slots.at[pl.ds(0, C * A - 1)], 0)
    left(first_slots.at[pl.ds(0, C * B - 1)], 1)
    left(terms_z.at[pl.ds(0, B - 1)], 2)
    left(grams_xy.at[pl.ds(0, A - 1)], 3)
    left(terms_xy.at[pl.ds(0, C * A - 1)], 4)
    left(half_in, 5)
    left(halves_z.at[pl.ds(0, B - 1)], 6)
    left(solved.at[0], 7)
    left(part_in, 8)
    left(raw_xy.at[pl.ds(0, A - 1)], 9)
    left(parts_xy.at[pl.ds(0, A - 1)], 10)
    left(norms.at[pl.ds(0, C * B - 1)], 11)


def share(counts, out, cells, first, second, sem):
    copies = [
        pltpu.make_async_copy(out.at[pl.ds(16 * n, counts[n])], target, sem.at[n])
        for n, target in enumerate((cells, first, second))
    ]
    for copy in copies:
        copy.start()
    for copy in copies:
        copy.wait()


def per_device(sizes, contacts, first_bins, second_bins):
    C, A, B, I, J, K = sizes
    cells, rows, columns = contacts.shape
    f32 = jnp.float32

    def tiles(*lead):
        return pltpu.VMEM(lead + (8, 128), f32)

    first_bins, second_bins = first_bins.T, second_bins.T
    out = (
        pl.pallas_call(
            functools.partial(kernel, sizes),
            out_shape=jax.ShapeDtypeStruct((cells + 32, R), f32),
            in_specs=[pl.BlockSpec(memory_space=pl.ANY)] * 3,
            out_specs=pl.BlockSpec(memory_space=pltpu.VMEM),
            scratch_shapes=[
                pltpu.VMEM((cells, rows, columns), f32),
                pltpu.VMEM((cells * rows, 2 * columns), jnp.bfloat16),
                pltpu.VMEM((2 * columns, cells * rows), jnp.bfloat16),
                pltpu.VMEM(first_bins.shape, f32),
                pltpu.VMEM(second_bins.shape, f32),
                pltpu.VMEM((128, 128), f32),
                pltpu.VMEM((C * B, 4, 128), f32),
                pltpu.VMEM((C * A, 4, 128), f32),
                tiles(B),
                tiles(A),
                pltpu.VMEM((C * A, 4, 128), f32),
                pltpu.VMEM((cells // 2, R, 2 * rows), f32),
                pltpu.VMEM((2, R, 128), f32),
                pltpu.VMEM((R, 128), f32),
                pltpu.VMEM((B, R, 128), f32),
                pltpu.VMEM((2, R, 128), f32),
                tiles(A),
                pltpu.VMEM((2, R + 16, 128), f32),
                pltpu.VMEM((R + 16, 128), f32),
                pltpu.VMEM((A, R + 16, 128), f32),
                pltpu.VMEM((C * B, 1, 128), f32),
                pltpu.VMEM((R, R, 128), f32),
                pltpu.SemaphoreType.DMA((2 + cells,)),
                pltpu.SemaphoreType.DMA((12,)),
                pltpu.SemaphoreType.DMA((12,)),
            ],
            compiler_params=pltpu.CompilerParams(
                collective_id=0, has_side_effects=True, vmem_limit_bytes=60 * 1024 * 1024
            ),
            name="sweep",
        )(contacts, first_bins, second_bins)
    )
    counts = (cells, first_bins.shape[0], second_bins.shape[0])
    shares = pl.pallas_call(
        functools.partial(share, counts),
        out_shape=tuple(jax.ShapeDtypeStruct((n, R), f32) for n in counts),
        in_specs=[pl.BlockSpec(memory_space=pl.ANY)],
        out_specs=[pl.BlockSpec(memory_space=pl.ANY)] * 3,
        scratch_shapes=[pltpu.SemaphoreType.DMA((3,))],
        name="share",
    )(out)
    return tuple(piece.T for piece in shares)


def solution(mesh):
    placed = (
        P("cell", "bini", "binj"),
        P(None, ("bini", "cell", "binj")),
        P(None, ("binj", "cell", "bini")),
    )

    def whole(contacts, first_bins, second_bins):
        sizes = (
            mesh.shape["cell"],
            mesh.shape["bini"],
            mesh.shape["binj"],
            contacts.shape[0],
            first_bins.shape[1],
            second_bins.shape[1],
        )
        return jax.shard_map(
            functools.partial(per_device, sizes),
            mesh=mesh,
            in_specs=placed,
            out_specs=(
                P(None, "cell"),
                P(None, ("bini", "cell", "binj")),
                P(None, ("binj", "cell", "bini")),
            ),
            check_vma=False,
        )(contacts, first_bins, second_bins)

    return whole
```

```python
import functools

import jax
import jax.numpy as jnp
from jax import lax
from jax.experimental import pallas as pl
from jax.experimental.pallas import tpu as pltpu
from jax.sharding import PartitionSpec as P

EPSILON = 1e-06
PRECISE = lax.Precision.HIGHEST
MESH = pl.DeviceIdType.MESH
R = 24
G = 3
SPREAD = 40
NT = (((1,), (1,)), ((), ()))


def lanes(shape):
    return lax.broadcasted_iota(jnp.int32, shape, 1)


def group(value, q):
    return value[8 * q : 8 * q + 8, :]


def stack(tiles):
    return jnp.concatenate(tiles, axis=0)


def turn(value, shift):
    if isinstance(shift, int):
        shift = shift % 128
        return value if shift == 0 else pltpu.roll(value, shift, 1)
    return pltpu.roll(value, shift, 1)


def pack(value, step, base=None):
    out = None
    for q in range(G):
        if base is None:
            tile = turn(group(value, q), step * q)
        else:
            tile = turn(group(value, q), lax.rem(base + step * q, 128))
        out = tile if out is None else out + tile
    return out


def unpack(tile, step, width, base=None):
    parts = []
    for q in range(G):
        if base is None:
            part = turn(tile, -step * q)
        else:
            part = turn(tile, lax.rem(256 - base - step * q, 128))
        parts.append(jnp.where(lanes(part.shape) < width, part, 0.0))
    return stack(parts)


def within(lane, start, width):
    return ((lane - start) & 127) < width


def spread(tile_at, count, width, tiles):
    lane = lanes((8, 128))
    wholes = []
    for v in range(count // 2):
        wholes.extend(whole_pair(tile_at(v), SPREAD // 2))
    out = [[jnp.zeros((8, 128), jnp.float32) for _ in range(tiles)] for _ in range(G)]
    for o in range(count):
        tile = wholes[o]
        start = width * o
        for t in range(tiles):
            low, high = max(start, 128 * t), min(start + width, 128 * t + 128)
            if low >= high:
                continue
            for q in range(G):
                mask = within(lane, (low + SPREAD * q) % 128, high - low)
                out[q][t] = jnp.where(mask, tile, out[q][t])
    return [stack([turn(out[q][t], -SPREAD * q) for q in range(G)]) for t in range(tiles)]


def swap(tile):
    return pltpu.roll(tile, 4, 0)


def two(slots, v):
    return jnp.concatenate([slots[2 * v], slots[2 * v + 1]], axis=0)


def halve(tile, step):
    return (tile + turn(swap(tile), step))[:4]


def whole_pair(tile, step):
    upper = lax.broadcasted_iota(jnp.int32, (8, 128), 0) < 4
    swapped = swap(tile)
    return jnp.where(upper, tile, turn(swapped, -step)), jnp.where(upper, swapped, turn(tile, -step))


def flip(value):
    tall = jnp.concatenate([value, jnp.zeros((128 - R, 128), jnp.float32)], axis=0)
    return tall.T[:, :R]


def split(value):
    high = value.astype(jnp.bfloat16)
    return high, (value - high.astype(jnp.float32)).astype(jnp.bfloat16)


def split_rows(value):
    high = value.astype(jnp.bfloat16).astype(jnp.float32)
    return jnp.concatenate([high, value - high], axis=0).astype(jnp.bfloat16)


def gram(tiles):
    total = None
    for tile in tiles:
        tall = jnp.concatenate([tile, jnp.zeros((128 - R, 128), jnp.float32)], axis=0)
        part = lax.dot_general(tile, tall, NT, precision=PRECISE, preferred_element_type=jnp.float32)
        total = part if total is None else total + part
    return total


def inverse(a):
    lane, row = lanes((R, 128)), lax.broadcasted_iota(jnp.int32, (R, 128), 0)
    for k in range(R):
        pivot_row = a[k : k + 1, :]
        pivot_column = a[:, k : k + 1]
        over = 1.0 / a[k : k + 1, k : k + 1]
        new_row = jnp.where(lane[:1] == k, over, pivot_row * over)
        a = jnp.where(lane == k, 0.0, a) - pivot_column * new_row
        a = jnp.where(row == k, new_row, a)
    return a


def widen(matrix, wide):
    for s in range(R):
        wide[s] = jnp.broadcast_to(matrix[:, s : s + 1], (R, 128))


def apply(wide, value):
    total = None
    for s in range(R):
        term = wide[s] * value[s : s + 1, :]
        total = term if total is None else total + term
    return total


def diagonal_scales(raw, count):
    lane, row = lanes((R, 128)), lax.broadcasted_iota(jnp.int32, (R, 128), 0)
    diagonal = jnp.where(lane == row, raw, 0.0)
    column = jnp.sum(diagonal, axis=1, keepdims=True)
    across = jnp.sum(diagonal, axis=0, keepdims=True)
    return jnp.sqrt(column / count + EPSILON), jnp.sqrt(across / count + EPSILON)


def kernel(
    sizes,
    contacts,
    first_in,
    second_in,
    out,
    x_full,
    x_parts,
    x_turned,
    first_land,
    second_land,
    pad,
    first_slots,
    second_slots,
    terms_z,
    grams_xy,
    terms_xy,
    products,
    halves,
    half_in,
    halves_z,
    solved,
    raw_xy,
    left_rows,
    parts,
    part_in,
    parts_xy,
    norms,
    wide_system,
    load_sem,
    send_sem,
    recv_sem,
):
    C, A, B, I, J, K = sizes
    cells, rows, columns = x_full.shape
    width_first, width_second = rows // (C * B), x_full.shape[2] // (C * A)
    c, a, b = lax.axis_index("cell"), lax.axis_index("bini"), lax.axis_index("binj")
    in_cz, in_cxy = c * B + b, c * A + a
    other = (1 - c, a, b)
    lane8, lane24 = lanes((8, 128)), lanes((R, 128))
    upper8 = lax.broadcasted_iota(jnp.int32, (8, 128), 0) < 4

    barrier = pltpu.get_barrier_semaphore()

    def signal(device):
        pl.semaphore_signal(barrier, inc=1, device_id=device, device_id_type=MESH)

    def flipped(m, size):
        first = size // 2 if size == B else size // 2 + size // 8
        m = m + first
        return jnp.where(m >= size, m - size + 1, m)

    def z_partner(m):
        return (c, a, b ^ flipped(m, B))

    def xy_partner(m):
        return (c, a ^ flipped(m, A), b)

    def across(device):
        return (1 - c, device[1], device[2])

    def over(count, partner, both, action):
        def one(m, carry):
            device = partner(m)
            action(device)
            if both:
                action(across(device))
            return carry

        lax.fori_loop(0, count - 1, one, 0)
        if both:
            action(other)

    z_partners, cz_partners = (B, z_partner, False), (B, z_partner, True)
    xy_partners, cxy_partners = (A, xy_partner, False), (A, xy_partner, True)
    over(*cz_partners, signal)
    over(A, xy_partner, False, signal)
    over(A, lambda m: across(xy_partner(m)), False, signal)

    loads = [
        pltpu.make_async_copy(second_in, second_land, load_sem.at[0]),
        pltpu.make_async_copy(first_in, first_land, load_sem.at[1]),
    ]
    for load in loads:
        load.start()

    def load_cell(i):
        return pltpu.make_async_copy(contacts.at[i], x_full.at[i], load_sem.at[2 + i])

    for i in range(cells):
        load_cell(i).start()

    pad[...] = jnp.zeros_like(pad)
    loads[0].wait()
    pad[:width_second, :R] = second_land[...]
    packed = pack(pad[...].T[:R], SPREAD, lax.rem(width_second * in_cxy, 128))
    second_slots[in_cxy] = halve(packed, SPREAD // 2)
    loads[1].wait()
    pad[:width_first, :R] = first_land[...]
    packed = pack(pad[...].T[:R], SPREAD, lax.rem(width_first * in_cz, 128))
    first_slots[in_cz] = halve(packed, SPREAD // 2)

    def send(source, target, number, device):
        pltpu.make_async_remote_copy(
            source, target, send_sem.at[number], recv_sem.at[number], device_id=device, device_id_type=MESH
        ).start()

    def send_all(source, target, number, partners):
        over(*partners, lambda device: send(source, target, number, device))

    def arrived(like, number):
        pltpu.make_async_copy(like, like, recv_sem.at[number]).wait()

    def left(like, number):
        pltpu.make_async_copy(like, like, send_sem.at[number]).wait()

    def split_pair(p, carry):
        load_cell(2 * p).wait()
        load_cell(2 * p + 1).wait()
        pair = x_full[pl.ds(2 * p, 2)].reshape(2 * rows, columns)
        at = pl.ds(pl.multiple_of(2 * rows * p, 2 * rows), 2 * rows)
        high = pair.astype(jnp.bfloat16).astype(jnp.float32)
        low = pair - high
        half = columns // 2
        x_parts[at, :columns] = jnp.concatenate([high[:, :half], low[:, :half]], axis=1).astype(jnp.bfloat16)
        x_parts[at, columns:] = jnp.concatenate([high[:, half:], low[:, half:]], axis=1).astype(jnp.bfloat16)
        x_turned[:columns, at], x_turned[columns:, at] = split(pair.T)
        return carry

    pl.semaphore_wait(barrier, C * B - 1 + C * (A - 1))

    mine = second_slots.at[in_cxy]
    send_all(mine, mine, 0, cxy_partners)
    mine = first_slots.at[in_cz]
    send_all(mine, mine, 1, cz_partners)
    lax.fori_loop(0, cells // 2, split_pair, 0)

    arrived(second_slots.at[pl.ds(0, C * A - 1)], 0)
    second = spread(lambda v: two(second_slots, v), C * A, width_second, 3)
    second_rows = split_rows(jnp.concatenate(second, axis=1))
    second_rows = jnp.concatenate([second_rows, second_rows], axis=1)
    arrived(first_slots.at[pl.ds(0, C * B - 1)], 1)
    first = spread(lambda v: two(first_slots, v), C * B, width_first, 2)
    first_turned = [turn(group(first[0], q), 64) for q in range(G)]
    first_turned = stack(first_turned)
    last_turned = stack([turn(group(first[1], q), 64) for q in range(G)])
    first_pair = [
        first[0],
        jnp.where(lane24 < 64, first[1], first_turned),
        jnp.where(lane24 < 64, first_turned, last_turned),
    ]

    cell_terms = jnp.zeros((R, 128), jnp.float32)
    for p in range(cells // 2):
        if p % 2 == 0:
            at = pl.ds(2 * rows * p, 4 * rows)
            wide = jnp.dot(second_rows, x_turned[:, at], preferred_element_type=jnp.float32)
            wide = wide[:R] + wide[R:]
        both = wide[:, 2 * rows * (p % 2) : 2 * rows * (p % 2 + 1)]
        products[p] = both
        terms = [both[:, 128 * t : 128 * t + 128] * first_pair[t] for t in range(3)]
        even = jnp.sum(terms[0] + jnp.where(lane24 < 64, terms[1], 0.0), axis=1, keepdims=True)
        odd = jnp.sum(terms[2] + jnp.where(lane24 < 64, 0.0, terms[1]), axis=1, keepdims=True)
        cell_terms = jnp.where(lane24 == 2 * p, even, cell_terms)
        cell_terms = jnp.where(lane24 == 2 * p + 1, odd, cell_terms)

    terms_z[b] = pack(cell_terms, cells) + turn(pack(gram(second), R), 56)
    mine = terms_z.at[b]
    send_all(mine, mine, 2, z_partners)
    grams_xy[a] = pack(gram(first), R)
    mine = grams_xy.at[a]
    send_all(mine, mine, 3, xy_partners)

    arrived(terms_z.at[pl.ds(0, B - 1)], 2)
    summed = terms_z[0]
    for o in range(1, B):
        summed = summed + terms_z[o]
    terms_xy[in_cxy] = halve(jnp.where(lane8 < G * cells, summed, 0.0), G * cells)
    mine = terms_xy.at[in_cxy]
    send_all(mine, mine, 4, cxy_partners)

    gram_second = unpack(turn(summed, -56), R, R)
    arrived(grams_xy.at[pl.ds(0, A - 1)], 3)
    summed = grams_xy[0]
    for o in range(1, A):
        summed = summed + grams_xy[o]
    gram_first = unpack(summed, R, R)
    widen(inverse(gram_first * gram_second), wide_system)

    arrived(terms_xy.at[pl.ds(0, C * A - 1)], 4)
    cell_total = None
    for core in range(C):
        summed = terms_xy[core * A]
        for o in range(1, A):
            summed = summed + terms_xy[core * A + o]
        summed = jnp.concatenate([summed, summed], axis=0)
        block = unpack(jnp.where(upper8, summed, turn(summed, -G * cells)), cells, cells)
        block = stack([turn(group(block, q), cells * core) for q in range(G)])
        cell_total = block if cell_total is None else cell_total + block

    unscaled = apply(wide_system, cell_total)
    scale = jnp.sqrt(jnp.sum(unscaled * unscaled, axis=1, keepdims=True) / I + EPSILON)
    cell_factor = unscaled / scale
    own_cells = stack([turn(group(cell_factor, q), lax.rem(128 - cells * c, 128)) for q in range(G)])

    pair_sum = [jnp.zeros((R, 128), jnp.float32) for _ in range(3)]
    weights = []
    for p in range(cells // 2):
        even = jnp.broadcast_to(own_cells[:, 2 * p : 2 * p + 1], (R, 128))
        odd = jnp.broadcast_to(own_cells[:, 2 * p + 1 : 2 * p + 2], (R, 128))
        weight = [even, jnp.where(lane24 < 64, even, odd), odd]
        weights.append(weight)
        both = products[p]
        for t in range(3):
            pair_sum[t] = pair_sum[t] + both[:, 128 * t : 128 * t + 128] * weight[t]

    def half_turn(value):
        return stack([turn(group(value, q), 64) for q in range(G)])

    turned = [half_turn(pair_sum[1]), half_turn(pair_sum[2])]
    halves[0] = pair_sum[0] + jnp.where(lane24 < 64, turned[0], turned[1])
    halves[1] = jnp.where(lane24 < 64, pair_sum[1] + turned[1], 0.0)
    send(halves.at[1 - c], half_in, 5, other)

    arrived(half_in, 5)
    halves_z[b] = halves[c] + half_in[...]
    mine = halves_z.at[b]
    send_all(mine, mine, 6, z_partners)
    raw = gram([unscaled])
    scale_column, scale_row = diagonal_scales(raw, I)
    gram_cells = jnp.where(lane24 < R, raw / (scale_column * scale_row), 0.0)
    out[:cells, :] = flip(own_cells)[:cells]
    widen(inverse(gram_cells * gram_second), wide_system)
    arrived(halves_z.at[pl.ds(0, B - 1)], 6)
    summed = halves_z[0]
    for o in range(1, B):
        summed = summed + halves_z[o]
    solved[c] = apply(wide_system, summed)
    mine = solved.at[c]
    send(mine, mine, 7, other)
    arrived(solved.at[0], 7)
    low, high = solved[0], solved[1]
    raw_xy[a] = pack(gram([low, high]), R)

    low_turned, high_turned = half_turn(low), half_turn(high)
    solved_pair = [
        low,
        jnp.where(lane24 < 64, high, low_turned),
        jnp.where(lane24 < 64, low_turned, high_turned),
    ]
    for p in range(0, cells // 2, 2):
        left_rows[:, 2 * rows * p : 2 * rows * (p + 2)] = split_rows(
            jnp.concatenate([solved_pair[t] * weights[p + h][t] for h in range(2) for t in range(3)], axis=1)
        )

    def second_pass(core):
        at = pl.ds(pl.multiple_of(columns * core, columns), columns)
        total = None
        for p in range(0, cells // 2, 2):
            here = pl.ds(2 * rows * p, 4 * rows)
            both = jnp.dot(left_rows[:, here], x_parts[here, at], preferred_element_type=jnp.float32)
            total = both if total is None else total + both
        total = total[:R] + total[R:]
        first, middle, last = [total[:, 128 * t : 128 * t + 128] for t in range(3)]
        middle, last = half_turn(middle), half_turn(last)
        low = first + jnp.where(lane24 < 64, middle, last)
        high = jnp.where(lane24 < 64, total[:, 128:256] + last, 0.0)
        return jnp.concatenate([low, group(high, 0) + turn(group(high, 1), 64), group(high, 2)], axis=0)

    parts[...] = second_pass(1 - c)
    send(parts, part_in, 8, other)
    mine = raw_xy.at[a]
    send_all(mine, mine, 9, xy_partners)
    own_part = second_pass(c)
    arrived(part_in, 8)
    parts_xy[a] = own_part + part_in[...]
    mine = parts_xy.at[a]
    send_all(mine, mine, 10, xy_partners)

    arrived(raw_xy.at[pl.ds(0, A - 1)], 9)
    summed = raw_xy[0]
    for o in range(1, A):
        summed = summed + raw_xy[o]
    raw = unpack(summed, R, R)
    scale_column, scale_row = diagonal_scales(raw, J)
    gram_first = jnp.where(lane24 < R, raw / (scale_column * scale_row), 0.0)
    widen(inverse(gram_cells * gram_first) / scale_row, wide_system)
    start = width_first * in_cz
    at_low = lax.rem(256 - start, 128)
    piece = [
        jnp.where(lane8 < 128 - start, turn(group(solved[0], q), at_low), turn(group(solved[1], q), at_low))
        for q in range(G)
    ]
    out[cells : cells + width_first, :] = flip(stack(piece) / scale_column)[:width_first]

    arrived(parts_xy.at[pl.ds(0, A - 1)], 10)
    summed = parts_xy[0]
    for o in range(1, A):
        summed = summed + parts_xy[o]
    mixed = summed[R : R + 8]
    low = summed[:R]
    high = [jnp.where(lane8 < 64, mixed, 0.0), jnp.where(lane8 < 64, turn(mixed, 64), 0.0), summed[R + 8 :]]
    low, high = apply(wide_system, low), apply(wide_system, stack(high))

    norm = jnp.sum(low * low + high * high, axis=1, keepdims=True)
    row24 = lax.broadcasted_iota(jnp.int32, (R, 128), 0)
    norms[in_cz] = jnp.sum(jnp.where(lane24 == row24, norm, 0.0), axis=0, keepdims=True)
    mine = norms.at[in_cz]
    send_all(mine, mine, 11, cz_partners)
    start = width_second * a
    at_low = lax.rem(256 - start, 128)
    piece = [
        jnp.where(lane8 < 128 - start, turn(group(low, q), at_low), turn(group(high, q), at_low))
        for q in range(G)
    ]
    piece = flip(stack(piece))[:width_second]
    arrived(norms.at[pl.ds(0, C * B - 1)], 11)
    norm = norms[0]
    for o in range(1, C * B):
        norm = norm + norms[o]
    out[cells + 16 : cells + 16 + width_second, :] = piece / jnp.sqrt(norm / K + EPSILON)[:, :R]

    left(second_slots.at[pl.ds(0, C * A - 1)], 0)
    left(first_slots.at[pl.ds(0, C * B - 1)], 1)
    left(terms_z.at[pl.ds(0, B - 1)], 2)
    left(grams_xy.at[pl.ds(0, A - 1)], 3)
    left(terms_xy.at[pl.ds(0, C * A - 1)], 4)
    left(half_in, 5)
    left(halves_z.at[pl.ds(0, B - 1)], 6)
    left(solved.at[0], 7)
    left(part_in, 8)
    left(raw_xy.at[pl.ds(0, A - 1)], 9)
    left(parts_xy.at[pl.ds(0, A - 1)], 10)
    left(norms.at[pl.ds(0, C * B - 1)], 11)


def share(counts, out, cells, first, second, sem):
    copies = [
        pltpu.make_async_copy(out.at[pl.ds(16 * n, counts[n])], target, sem.at[n])
        for n, target in enumerate((cells, first, second))
    ]
    for copy in copies:
        copy.start()
    for copy in copies:
        copy.wait()


def per_device(sizes, contacts, first_bins, second_bins):
    C, A, B, I, J, K = sizes
    cells, rows, columns = contacts.shape
    f32 = jnp.float32

    def tiles(*lead):
        return pltpu.VMEM(lead + (8, 128), f32)

    first_bins, second_bins = first_bins.T, second_bins.T
    out = (
        pl.pallas_call(
            functools.partial(kernel, sizes),
            out_shape=jax.ShapeDtypeStruct((cells + 32, R), f32),
            in_specs=[pl.BlockSpec(memory_space=pl.ANY)] * 3,
            out_specs=pl.BlockSpec(memory_space=pltpu.VMEM),
            scratch_shapes=[
                pltpu.VMEM((cells, rows, columns), f32),
                pltpu.VMEM((cells * rows, 2 * columns), jnp.bfloat16),
                pltpu.VMEM((2 * columns, cells * rows), jnp.bfloat16),
                pltpu.VMEM(first_bins.shape, f32),
                pltpu.VMEM(second_bins.shape, f32),
                pltpu.VMEM((128, 128), f32),
                pltpu.VMEM((C * B, 4, 128), f32),
                pltpu.VMEM((C * A, 4, 128), f32),
                tiles(B),
                tiles(A),
                pltpu.VMEM((C * A, 4, 128), f32),
                pltpu.VMEM((cells // 2, R, 2 * rows), f32),
                pltpu.VMEM((2, R, 128), f32),
                pltpu.VMEM((R, 128), f32),
                pltpu.VMEM((B, R, 128), f32),
                pltpu.VMEM((2, R, 128), f32),
                tiles(A),
                pltpu.VMEM((2 * R, cells * rows), jnp.bfloat16),
                pltpu.VMEM((R + 16, 128), f32),
                pltpu.VMEM((R + 16, 128), f32),
                pltpu.VMEM((A, R + 16, 128), f32),
                pltpu.VMEM((C * B, 1, 128), f32),
                pltpu.VMEM((R, R, 128), f32),
                pltpu.SemaphoreType.DMA((2 + cells,)),
                pltpu.SemaphoreType.DMA((12,)),
                pltpu.SemaphoreType.DMA((12,)),
            ],
            compiler_params=pltpu.CompilerParams(
                collective_id=0, has_side_effects=True, vmem_limit_bytes=60 * 1024 * 1024
            ),
            name="sweep",
        )(contacts, first_bins, second_bins)
    )
    counts = (cells, first_bins.shape[0], second_bins.shape[0])
    shares = pl.pallas_call(
        functools.partial(share, counts),
        out_shape=tuple(jax.ShapeDtypeStruct((n, R), f32) for n in counts),
        in_specs=[pl.BlockSpec(memory_space=pl.ANY)],
        out_specs=[pl.BlockSpec(memory_space=pl.ANY)] * 3,
        scratch_shapes=[pltpu.SemaphoreType.DMA((3,))],
        name="share",
    )(out)
    return tuple(piece.T for piece in shares)


def solution(mesh):
    placed = (
        P("cell", "bini", "binj"),
        P(None, ("bini", "cell", "binj")),
        P(None, ("binj", "cell", "bini")),
    )

    def whole(contacts, first_bins, second_bins):
        sizes = (
            mesh.shape["cell"],
            mesh.shape["bini"],
            mesh.shape["binj"],
            contacts.shape[0],
            first_bins.shape[1],
            second_bins.shape[1],
        )
        return jax.shard_map(
            functools.partial(per_device, sizes),
            mesh=mesh,
            in_specs=placed,
            out_specs=(
                P(None, "cell"),
                P(None, ("bini", "cell", "binj")),
                P(None, ("binj", "cell", "bini")),
            ),
            check_vma=False,
        )(contacts, first_bins, second_bins)

    return whole
```

```python
import functools

import jax
import jax.numpy as jnp
from jax import lax
from jax.experimental import pallas as pl
from jax.experimental.pallas import tpu as pltpu
from jax.sharding import PartitionSpec as P

EPSILON = 1e-06
PRECISE = lax.Precision.HIGHEST
MESH = pl.DeviceIdType.MESH
R = 24
G = 3
SPREAD = 40
NT = (((1,), (1,)), ((), ()))


def lanes(shape):
    return lax.broadcasted_iota(jnp.int32, shape, 1)


def group(value, q):
    return value[8 * q : 8 * q + 8, :]


def stack(tiles):
    return jnp.concatenate(tiles, axis=0)


def turn(value, shift):
    if isinstance(shift, int):
        shift = shift % 128
        return value if shift == 0 else pltpu.roll(value, shift, 1)
    return pltpu.roll(value, shift, 1)


def pack(value, step, base=None):
    out = None
    for q in range(G):
        if base is None:
            tile = turn(group(value, q), step * q)
        else:
            tile = turn(group(value, q), lax.rem(base + step * q, 128))
        out = tile if out is None else out + tile
    return out


def unpack(tile, step, width, base=None):
    parts = []
    for q in range(G):
        if base is None:
            part = turn(tile, -step * q)
        else:
            part = turn(tile, lax.rem(256 - base - step * q, 128))
        parts.append(jnp.where(lanes(part.shape) < width, part, 0.0))
    return stack(parts)


def within(lane, start, width):
    return ((lane - start) & 127) < width


def spread(tile_at, count, width, tiles):
    lane = lanes((8, 128))
    wholes = []
    for v in range(count // 2):
        wholes.extend(whole_pair(tile_at(v), SPREAD // 2))
    out = [[jnp.zeros((8, 128), jnp.float32) for _ in range(tiles)] for _ in range(G)]
    for o in range(count):
        tile = wholes[o]
        start = width * o
        for t in range(tiles):
            low, high = max(start, 128 * t), min(start + width, 128 * t + 128)
            if low >= high:
                continue
            for q in range(G):
                mask = within(lane, (low + SPREAD * q) % 128, high - low)
                out[q][t] = jnp.where(mask, tile, out[q][t])
    return [stack([turn(out[q][t], -SPREAD * q) for q in range(G)]) for t in range(tiles)]


def swap(tile):
    return pltpu.roll(tile, 4, 0)


def two(slots, v):
    return jnp.concatenate([slots[2 * v], slots[2 * v + 1]], axis=0)


def halve(tile, step):
    return (tile + turn(swap(tile), step))[:4]


def whole_pair(tile, step):
    upper = lax.broadcasted_iota(jnp.int32, (8, 128), 0) < 4
    swapped = swap(tile)
    return jnp.where(upper, tile, turn(swapped, -step)), jnp.where(upper, swapped, turn(tile, -step))


def flip(value):
    tall = jnp.concatenate([value, jnp.zeros((128 - R, 128), jnp.float32)], axis=0)
    return tall.T[:, :R]


def split(value):
    high = value.astype(jnp.bfloat16)
    return high, (value - high.astype(jnp.float32)).astype(jnp.bfloat16)


def split_rows(value):
    high = value.astype(jnp.bfloat16).astype(jnp.float32)
    return jnp.concatenate([high, value - high], axis=0).astype(jnp.bfloat16)


def gram(tiles):
    total = None
    for tile in tiles:
        tall = jnp.concatenate([tile, jnp.zeros((128 - R, 128), jnp.float32)], axis=0)
        part = lax.dot_general(tile, tall, NT, precision=PRECISE, preferred_element_type=jnp.float32)
        total = part if total is None else total + part
    return total


def inverse(a):
    lane, row = lanes((R, 128)), lax.broadcasted_iota(jnp.int32, (R, 128), 0)
    for k in range(R):
        pivot_row = a[k : k + 1, :]
        pivot_column = a[:, k : k + 1]
        over = 1.0 / a[k : k + 1, k : k + 1]
        new_row = jnp.where(lane[:1] == k, over, pivot_row * over)
        a = jnp.where(lane == k, 0.0, a) - pivot_column * new_row
        a = jnp.where(row == k, new_row, a)
    return a


def widen(matrix, wide):
    for s in range(R):
        wide[s] = jnp.broadcast_to(matrix[:, s : s + 1], (R, 128))


def apply(wide, value):
    total = None
    for s in range(R):
        term = wide[s] * value[s : s + 1, :]
        total = term if total is None else total + term
    return total


def diagonal_scales(raw, count):
    lane, row = lanes((R, 128)), lax.broadcasted_iota(jnp.int32, (R, 128), 0)
    diagonal = jnp.where(lane == row, raw, 0.0)
    column = jnp.sum(diagonal, axis=1, keepdims=True)
    across = jnp.sum(diagonal, axis=0, keepdims=True)
    return jnp.sqrt(column / count + EPSILON), jnp.sqrt(across / count + EPSILON)


def kernel(
    sizes,
    contacts,
    first_in,
    second_in,
    out,
    x_full,
    x_parts,
    x_turned,
    first_land,
    second_land,
    pad,
    first_slots,
    second_slots,
    terms_z,
    grams_xy,
    terms_xy,
    products,
    halves,
    half_in,
    halves_z,
    solved,
    raw_xy,
    left_rows,
    parts,
    part_in,
    parts_xy,
    norms,
    wide_system,
    load_sem,
    send_sem,
    recv_sem,
):
    C, A, B, I, J, K = sizes
    cells, rows, columns = x_full.shape
    width_first, width_second = rows // (C * B), x_full.shape[2] // (C * A)
    c, a, b = lax.axis_index("cell"), lax.axis_index("bini"), lax.axis_index("binj")
    in_cz, in_cxy = c * B + b, c * A + a
    other = (1 - c, a, b)
    lane8, lane24 = lanes((8, 128)), lanes((R, 128))
    upper8 = lax.broadcasted_iota(jnp.int32, (8, 128), 0) < 4

    barrier = pltpu.get_barrier_semaphore()

    def signal(device):
        pl.semaphore_signal(barrier, inc=1, device_id=device, device_id_type=MESH)

    def flipped(m, size):
        first = size // 2 if size == B else size // 2 + size // 8
        m = m + first
        return jnp.where(m >= size, m - size + 1, m)

    def z_partner(m):
        return (c, a, b ^ flipped(m, B))

    def xy_partner(m):
        return (c, a ^ flipped(m, A), b)

    def across(device):
        return (1 - c, device[1], device[2])

    def over(count, partner, both, action):
        def one(m, carry):
            device = partner(m)
            action(device)
            if both:
                action(across(device))
            return carry

        lax.fori_loop(0, count - 1, one, 0)
        if both:
            action(other)

    z_partners, cz_partners = (B, z_partner, False), (B, z_partner, True)
    xy_partners, cxy_partners = (A, xy_partner, False), (A, xy_partner, True)
    over(*cz_partners, signal)
    over(A, xy_partner, False, signal)
    over(A, lambda m: across(xy_partner(m)), False, signal)

    loads = [
        pltpu.make_async_copy(second_in, second_land, load_sem.at[0]),
        pltpu.make_async_copy(first_in, first_land, load_sem.at[1]),
    ]
    for load in loads:
        load.start()

    def load_cell(i):
        return pltpu.make_async_copy(contacts.at[i], x_full.at[i], load_sem.at[2 + i])

    for i in range(cells):
        load_cell(i).start()

    pad[...] = jnp.zeros_like(pad)
    loads[0].wait()
    pad[:width_second, :R] = second_land[...]
    packed = pack(pad[...].T[:R], SPREAD, lax.rem(width_second * in_cxy, 128))
    second_slots[in_cxy] = halve(packed, SPREAD // 2)
    loads[1].wait()
    pad[:width_first, :R] = first_land[...]
    packed = pack(pad[...].T[:R], SPREAD, lax.rem(width_first * in_cz, 128))
    first_slots[in_cz] = halve(packed, SPREAD // 2)

    def send(source, target, number, device):
        pltpu.make_async_remote_copy(
            source, target, send_sem.at[number], recv_sem.at[number], device_id=device, device_id_type=MESH
        ).start()

    def send_all(source, target, number, partners):
        over(*partners, lambda device: send(source, target, number, device))

    def arrived(like, number):
        pltpu.make_async_copy(like, like, recv_sem.at[number]).wait()

    def left(like, number):
        pltpu.make_async_copy(like, like, send_sem.at[number]).wait()

    def split_pair(p, carry):
        load_cell(2 * p).wait()
        load_cell(2 * p + 1).wait()
        pair = x_full[pl.ds(2 * p, 2)].reshape(2 * rows, columns)
        at = pl.ds(pl.multiple_of(2 * rows * p, 2 * rows), 2 * rows)
        high = pair.astype(jnp.bfloat16).astype(jnp.float32)
        low = pair - high
        half = columns // 2
        x_parts[at, :columns] = jnp.concatenate([high[:, :half], low[:, :half]], axis=1).astype(jnp.bfloat16)
        x_parts[at, columns:] = jnp.concatenate([high[:, half:], low[:, half:]], axis=1).astype(jnp.bfloat16)
        x_turned[:columns, at], x_turned[columns:, at] = split(pair.T)
        return carry

    pl.semaphore_wait(barrier, C * B - 1 + C * (A - 1))

    mine = second_slots.at[in_cxy]
    send_all(mine, mine, 0, cxy_partners)
    mine = first_slots.at[in_cz]
    send_all(mine, mine, 1, cz_partners)
    lax.fori_loop(0, cells // 2, split_pair, 0)

    arrived(second_slots.at[pl.ds(0, C * A - 1)], 0)
    second = spread(lambda v: two(second_slots, v), C * A, width_second, 3)
    second_rows = split_rows(jnp.concatenate(second, axis=1))
    second_rows = jnp.concatenate([second_rows, second_rows], axis=1)
    arrived(first_slots.at[pl.ds(0, C * B - 1)], 1)
    first = spread(lambda v: two(first_slots, v), C * B, width_first, 2)
    first_turned = [turn(group(first[0], q), 64) for q in range(G)]
    first_turned = stack(first_turned)
    last_turned = stack([turn(group(first[1], q), 64) for q in range(G)])
    first_pair = [
        first[0],
        jnp.where(lane24 < 64, first[1], first_turned),
        jnp.where(lane24 < 64, first_turned, last_turned),
    ]

    cell_terms = jnp.zeros((R, 128), jnp.float32)
    for p in range(cells // 2):
        if p % 2 == 0:
            at = pl.ds(2 * rows * p, 4 * rows)
            wide = jnp.dot(second_rows, x_turned[:, at], preferred_element_type=jnp.float32)
            wide = wide[:R] + wide[R:]
        both = wide[:, 2 * rows * (p % 2) : 2 * rows * (p % 2 + 1)]
        products[p] = both
        terms = [both[:, 128 * t : 128 * t + 128] * first_pair[t] for t in range(3)]
        even = jnp.sum(terms[0] + jnp.where(lane24 < 64, terms[1], 0.0), axis=1, keepdims=True)
        odd = jnp.sum(terms[2] + jnp.where(lane24 < 64, 0.0, terms[1]), axis=1, keepdims=True)
        cell_terms = jnp.where(lane24 == 2 * p, even, cell_terms)
        cell_terms = jnp.where(lane24 == 2 * p + 1, odd, cell_terms)

    terms_z[b] = pack(cell_terms, cells) + turn(pack(gram(second), R), 56)
    mine = terms_z.at[b]
    send_all(mine, mine, 2, z_partners)
    grams_xy[a] = pack(gram(first), R)
    mine = grams_xy.at[a]
    send_all(mine, mine, 3, xy_partners)

    arrived(terms_z.at[pl.ds(0, B - 1)], 2)
    summed = terms_z[0]
    for o in range(1, B):
        summed = summed + terms_z[o]
    terms_xy[in_cxy] = halve(jnp.where(lane8 < G * cells, summed, 0.0), G * cells)
    mine = terms_xy.at[in_cxy]
    send_all(mine, mine, 4, cxy_partners)

    gram_second = unpack(turn(summed, -56), R, R)
    arrived(grams_xy.at[pl.ds(0, A - 1)], 3)
    summed = grams_xy[0]
    for o in range(1, A):
        summed = summed + grams_xy[o]
    gram_first = unpack(summed, R, R)
    widen(inverse(gram_first * gram_second), wide_system)

    arrived(terms_xy.at[pl.ds(0, C * A - 1)], 4)
    cell_total = None
    for core in range(C):
        summed = terms_xy[core * A]
        for o in range(1, A):
            summed = summed + terms_xy[core * A + o]
        summed = jnp.concatenate([summed, summed], axis=0)
        block = unpack(jnp.where(upper8, summed, turn(summed, -G * cells)), cells, cells)
        block = stack([turn(group(block, q), cells * core) for q in range(G)])
        cell_total = block if cell_total is None else cell_total + block

    unscaled = apply(wide_system, cell_total)
    scale = jnp.sqrt(jnp.sum(unscaled * unscaled, axis=1, keepdims=True) / I + EPSILON)
    cell_factor = unscaled / scale
    own_cells = stack([turn(group(cell_factor, q), lax.rem(128 - cells * c, 128)) for q in range(G)])

    pair_sum = [jnp.zeros((R, 128), jnp.float32) for _ in range(3)]
    weights = []
    for p in range(cells // 2):
        even = jnp.broadcast_to(own_cells[:, 2 * p : 2 * p + 1], (R, 128))
        odd = jnp.broadcast_to(own_cells[:, 2 * p + 1 : 2 * p + 2], (R, 128))
        weight = [even, jnp.where(lane24 < 64, even, odd), odd]
        weights.append(weight)
        both = products[p]
        for t in range(3):
            pair_sum[t] = pair_sum[t] + both[:, 128 * t : 128 * t + 128] * weight[t]

    def half_turn(value):
        return stack([turn(group(value, q), 64) for q in range(G)])

    turned = [half_turn(pair_sum[1]), half_turn(pair_sum[2])]
    halves[0] = pair_sum[0] + jnp.where(lane24 < 64, turned[0], turned[1])
    halves[1] = jnp.where(lane24 < 64, pair_sum[1] + turned[1], 0.0)
    send(halves.at[1 - c], half_in, 5, other)

    arrived(half_in, 5)
    halves_z[b] = halves[c] + half_in[...]
    mine = halves_z.at[b]
    send_all(mine, mine, 6, z_partners)
    raw = gram([unscaled])
    scale_column, scale_row = diagonal_scales(raw, I)
    gram_cells = jnp.where(lane24 < R, raw / (scale_column * scale_row), 0.0)
    out[:cells, :] = flip(own_cells)[:cells]
    widen(inverse(gram_cells * gram_second), wide_system)
    arrived(halves_z.at[pl.ds(0, B - 1)], 6)
    summed = halves_z[0]
    for o in range(1, B):
        summed = summed + halves_z[o]
    solved[c] = apply(wide_system, summed)
    mine = solved.at[c]
    send(mine, mine, 7, other)
    arrived(solved.at[0], 7)
    low, high = solved[0], solved[1]
    raw_xy[a] = pack(gram([low, high]), R)

    low_turned, high_turned = half_turn(low), half_turn(high)
    solved_pair = [
        low,
        jnp.where(lane24 < 64, high, low_turned),
        jnp.where(lane24 < 64, low_turned, high_turned),
    ]
    for p in range(0, cells // 2, 2):
        left_rows[:, 2 * rows * p : 2 * rows * (p + 2)] = split_rows(
            jnp.concatenate([solved_pair[t] * weights[p + h][t] for h in range(2) for t in range(3)], axis=1)
        )

    def second_pass(core):
        at = pl.ds(pl.multiple_of(columns * core, columns), columns)
        total = None
        for p in range(0, cells // 2, 2):
            here = pl.ds(2 * rows * p, 4 * rows)
            both = jnp.dot(left_rows[:, here], x_parts[here, at], preferred_element_type=jnp.float32)
            total = both if total is None else total + both
        total = total[:R] + total[R:]
        first, middle, last = [total[:, 128 * t : 128 * t + 128] for t in range(3)]
        middle, last = half_turn(middle), half_turn(last)
        low = first + jnp.where(lane24 < 64, middle, last)
        high = jnp.where(lane24 < 64, total[:, 128:256] + last, 0.0)
        return jnp.concatenate([low, group(high, 0) + turn(group(high, 1), 64), group(high, 2)], axis=0)

    parts[...] = second_pass(1 - c)
    send(parts, part_in, 8, other)
    mine = raw_xy.at[a]
    send_all(mine, mine, 9, xy_partners)
    own_part = second_pass(c)
    arrived(part_in, 8)
    parts_xy[a] = own_part + part_in[...]
    mine = parts_xy.at[a]
    send_all(mine, mine, 10, xy_partners)

    arrived(raw_xy.at[pl.ds(0, A - 1)], 9)
    summed = raw_xy[0]
    for o in range(1, A):
        summed = summed + raw_xy[o]
    raw = unpack(summed, R, R)
    scale_column, scale_row = diagonal_scales(raw, J)
    gram_first = jnp.where(lane24 < R, raw / (scale_column * scale_row), 0.0)
    widen(inverse(gram_cells * gram_first) / scale_row, wide_system)
    start = width_first * in_cz
    at_low = lax.rem(256 - start, 128)
    piece = [
        jnp.where(lane8 < 128 - start, turn(group(solved[0], q), at_low), turn(group(solved[1], q), at_low))
        for q in range(G)
    ]
    out[cells : cells + width_first, :] = flip(stack(piece) / scale_column)[:width_first]

    arrived(parts_xy.at[pl.ds(0, A - 1)], 10)
    summed = parts_xy[0]
    for o in range(1, A):
        summed = summed + parts_xy[o]
    mixed = summed[R : R + 8]
    low = summed[:R]
    high = [jnp.where(lane8 < 64, mixed, 0.0), jnp.where(lane8 < 64, turn(mixed, 64), 0.0), summed[R + 8 :]]
    low, high = apply(wide_system, low), apply(wide_system, stack(high))

    norm = jnp.sum(low * low + high * high, axis=1, keepdims=True)
    row24 = lax.broadcasted_iota(jnp.int32, (R, 128), 0)
    norms[in_cz] = jnp.sum(jnp.where(lane24 == row24, norm, 0.0), axis=0, keepdims=True)
    mine = norms.at[in_cz]
    send_all(mine, mine, 11, cz_partners)
    start = width_second * a
    at_low = lax.rem(256 - start, 128)
    piece = [
        jnp.where(lane8 < 128 - start, turn(group(low, q), at_low), turn(group(high, q), at_low))
        for q in range(G)
    ]
    piece = flip(stack(piece))[:width_second]
    arrived(norms.at[pl.ds(0, C * B - 1)], 11)
    norm = norms[0]
    for o in range(1, C * B):
        norm = norm + norms[o]
    out[cells + 16 : cells + 16 + width_second, :] = piece / jnp.sqrt(norm / K + EPSILON)[:, :R]

    left(second_slots.at[pl.ds(0, C * A - 1)], 0)
    left(first_slots.at[pl.ds(0, C * B - 1)], 1)
    left(terms_z.at[pl.ds(0, B - 1)], 2)
    left(grams_xy.at[pl.ds(0, A - 1)], 3)
    left(terms_xy.at[pl.ds(0, C * A - 1)], 4)
    left(half_in, 5)
    left(halves_z.at[pl.ds(0, B - 1)], 6)
    left(solved.at[0], 7)
    left(part_in, 8)
    left(raw_xy.at[pl.ds(0, A - 1)], 9)
    left(parts_xy.at[pl.ds(0, A - 1)], 10)
    left(norms.at[pl.ds(0, C * B - 1)], 11)


def share(counts, out, cells, first, second, sem):
    copies = [
        pltpu.make_async_copy(out.at[pl.ds(16 * n, counts[n])], target, sem.at[n])
        for n, target in enumerate((cells, first, second))
    ]
    for copy in copies:
        copy.start()
    for copy in copies:
        copy.wait()


def per_device(sizes, contacts, first_bins, second_bins):
    C, A, B, I, J, K = sizes
    cells, rows, columns = contacts.shape
    f32 = jnp.float32

    def tiles(*lead):
        return pltpu.VMEM(lead + (8, 128), f32)

    first_bins, second_bins = first_bins.T, second_bins.T
    out = (
        pl.pallas_call(
            functools.partial(kernel, sizes),
            out_shape=jax.ShapeDtypeStruct((cells + 32, R), f32),
            in_specs=[pl.BlockSpec(memory_space=pl.ANY)] * 3,
            out_specs=pl.BlockSpec(memory_space=pltpu.VMEM),
            scratch_shapes=[
                pltpu.VMEM((cells, rows, columns), f32),
                pltpu.VMEM((cells * rows, 2 * columns), jnp.bfloat16),
                pltpu.VMEM((2 * columns, cells * rows), jnp.bfloat16),
                pltpu.VMEM(first_bins.shape, f32),
                pltpu.VMEM(second_bins.shape, f32),
                pltpu.VMEM((128, 128), f32),
                pltpu.VMEM((C * B, 4, 128), f32),
                pltpu.VMEM((C * A, 4, 128), f32),
                tiles(B),
                tiles(A),
                pltpu.VMEM((C * A, 4, 128), f32),
                pltpu.VMEM((cells // 2, R, 2 * rows), f32),
                pltpu.VMEM((2, R, 128), f32),
                pltpu.VMEM((R, 128), f32),
                pltpu.VMEM((B, R, 128), f32),
                pltpu.VMEM((2, R, 128), f32),
                tiles(A),
                pltpu.VMEM((2 * R, cells * rows), jnp.bfloat16),
                pltpu.VMEM((R + 16, 128), f32),
                pltpu.VMEM((R + 16, 128), f32),
                pltpu.VMEM((A, R + 16, 128), f32),
                pltpu.VMEM((C * B, 1, 128), f32),
                pltpu.VMEM((R, R, 128), f32),
                pltpu.SemaphoreType.DMA((2 + cells,)),
                pltpu.SemaphoreType.DMA((12,)),
                pltpu.SemaphoreType.DMA((12,)),
            ],
            compiler_params=pltpu.CompilerParams(
                collective_id=0, has_side_effects=True, vmem_limit_bytes=60 * 1024 * 1024
            ),
            name="sweep",
        )(contacts, first_bins, second_bins)
    )
    counts = (cells, first_bins.shape[0], second_bins.shape[0])
    shares = pl.pallas_call(
        functools.partial(share, counts),
        out_shape=tuple(jax.ShapeDtypeStruct((n, R), f32) for n in counts),
        in_specs=[pl.BlockSpec(memory_space=pltpu.VMEM)],
        out_specs=[pl.BlockSpec(memory_space=pl.ANY)] * 3,
        scratch_shapes=[pltpu.SemaphoreType.DMA((3,))],
        name="share",
    )(out)
    return tuple(piece.T for piece in shares)


def solution(mesh):
    placed = (
        P("cell", "bini", "binj"),
        P(None, ("bini", "cell", "binj")),
        P(None, ("binj", "cell", "bini")),
    )

    def whole(contacts, first_bins, second_bins):
        sizes = (
            mesh.shape["cell"],
            mesh.shape["bini"],
            mesh.shape["binj"],
            contacts.shape[0],
            first_bins.shape[1],
            second_bins.shape[1],
        )
        return jax.shard_map(
            functools.partial(per_device, sizes),
            mesh=mesh,
            in_specs=placed,
            out_specs=(
                P(None, "cell"),
                P(None, ("bini", "cell", "binj")),
                P(None, ("binj", "cell", "bini")),
            ),
            check_vma=False,
        )(contacts, first_bins, second_bins)

    return whole
```

```python
import functools

import jax
import jax.numpy as jnp
from jax import lax
from jax.experimental import pallas as pl
from jax.experimental.pallas import tpu as pltpu
from jax.sharding import PartitionSpec as P

EPSILON = 1e-06
PRECISE = lax.Precision.HIGHEST
MESH = pl.DeviceIdType.MESH
R = 24
G = 3
SPREAD = 40
NT = (((1,), (1,)), ((), ()))


def lanes(shape):
    return lax.broadcasted_iota(jnp.int32, shape, 1)


def group(value, q):
    return value[8 * q : 8 * q + 8, :]


def stack(tiles):
    return jnp.concatenate(tiles, axis=0)


def turn(value, shift):
    if isinstance(shift, int):
        shift = shift % 128
        return value if shift == 0 else pltpu.roll(value, shift, 1)
    return pltpu.roll(value, shift, 1)


def pack(value, step, base=None):
    out = None
    for q in range(G):
        if base is None:
            tile = turn(group(value, q), step * q)
        else:
            tile = turn(group(value, q), lax.rem(base + step * q, 128))
        out = tile if out is None else out + tile
    return out


def unpack(tile, step, width, base=None):
    parts = []
    for q in range(G):
        if base is None:
            part = turn(tile, -step * q)
        else:
            part = turn(tile, lax.rem(256 - base - step * q, 128))
        parts.append(jnp.where(lanes(part.shape) < width, part, 0.0))
    return stack(parts)


def within(lane, start, width):
    return ((lane - start) & 127) < width


def spread(tile_at, count, width, tiles):
    lane = lanes((8, 128))
    wholes = []
    for v in range(count // 2):
        wholes.extend(whole_pair(tile_at(v), SPREAD // 2))
    out = [[jnp.zeros((8, 128), jnp.float32) for _ in range(tiles)] for _ in range(G)]
    for o in range(count):
        tile = wholes[o]
        start = width * o
        for t in range(tiles):
            low, high = max(start, 128 * t), min(start + width, 128 * t + 128)
            if low >= high:
                continue
            for q in range(G):
                mask = within(lane, (low + SPREAD * q) % 128, high - low)
                out[q][t] = jnp.where(mask, tile, out[q][t])
    return [stack([turn(out[q][t], -SPREAD * q) for q in range(G)]) for t in range(tiles)]


def swap(tile):
    return pltpu.roll(tile, 4, 0)


def two(slots, v):
    return jnp.concatenate([slots[2 * v], slots[2 * v + 1]], axis=0)


def halve(tile, step):
    return (tile + turn(swap(tile), step))[:4]


def whole_pair(tile, step):
    upper = lax.broadcasted_iota(jnp.int32, (8, 128), 0) < 4
    swapped = swap(tile)
    return jnp.where(upper, tile, turn(swapped, -step)), jnp.where(upper, swapped, turn(tile, -step))


def flip(value):
    tall = jnp.concatenate([value, jnp.zeros((128 - R, 128), jnp.float32)], axis=0)
    return tall.T[:, :R]


def split(value):
    high = value.astype(jnp.bfloat16)
    return high, (value - high.astype(jnp.float32)).astype(jnp.bfloat16)


def split_rows(value):
    high = value.astype(jnp.bfloat16).astype(jnp.float32)
    return jnp.concatenate([high, value - high], axis=0).astype(jnp.bfloat16)


def gram(tiles):
    total = None
    for tile in tiles:
        tall = jnp.concatenate([tile, jnp.zeros((128 - R, 128), jnp.float32)], axis=0)
        part = lax.dot_general(tile, tall, NT, precision=PRECISE, preferred_element_type=jnp.float32)
        total = part if total is None else total + part
    return total


def inverse(a):
    lane, row = lanes((R, 128)), lax.broadcasted_iota(jnp.int32, (R, 128), 0)
    for k in range(R):
        pivot_row = a[k : k + 1, :]
        pivot_column = a[:, k : k + 1]
        over = 1.0 / a[k : k + 1, k : k + 1]
        new_row = jnp.where(lane[:1] == k, over, pivot_row * over)
        a = jnp.where(lane == k, 0.0, a) - pivot_column * new_row
        a = jnp.where(row == k, new_row, a)
    return a


def widen(matrix, wide):
    for s in range(R):
        wide[s] = jnp.broadcast_to(matrix[:, s : s + 1], (R, 128))


def apply(wide, value):
    total = None
    for s in range(R):
        term = wide[s] * value[s : s + 1, :]
        total = term if total is None else total + term
    return total


def diagonal_scales(raw, count):
    lane, row = lanes((R, 128)), lax.broadcasted_iota(jnp.int32, (R, 128), 0)
    diagonal = jnp.where(lane == row, raw, 0.0)
    column = jnp.sum(diagonal, axis=1, keepdims=True)
    across = jnp.sum(diagonal, axis=0, keepdims=True)
    return jnp.sqrt(column / count + EPSILON), jnp.sqrt(across / count + EPSILON)


def kernel(
    sizes,
    contacts,
    first_in,
    second_in,
    out,
    x_full,
    x_parts,
    x_turned,
    first_land,
    second_land,
    pad,
    first_slots,
    second_slots,
    terms_z,
    grams_xy,
    terms_xy,
    products,
    halves,
    half_in,
    halves_z,
    solved,
    raw_xy,
    left_rows,
    parts,
    part_in,
    parts_xy,
    norms,
    wide_system,
    load_sem,
    send_sem,
    recv_sem,
):
    C, A, B, I, J, K = sizes
    cells, rows, columns = x_full.shape
    width_first, width_second = rows // (C * B), x_full.shape[2] // (C * A)
    c, a, b = lax.axis_index("cell"), lax.axis_index("bini"), lax.axis_index("binj")
    in_cz, in_cxy = c * B + b, c * A + a
    other = (1 - c, a, b)
    lane8, lane24 = lanes((8, 128)), lanes((R, 128))
    upper8 = lax.broadcasted_iota(jnp.int32, (8, 128), 0) < 4

    barrier = pltpu.get_barrier_semaphore()

    def signal(device):
        pl.semaphore_signal(barrier, inc=1, device_id=device, device_id_type=MESH)

    def flipped(m, size):
        first = size // 2 if size == B else size // 2 + size // 8
        m = m + first
        return jnp.where(m >= size, m - size + 1, m)

    def z_partner(m):
        return (c, a, b ^ flipped(m, B))

    def xy_partner(m):
        return (c, a ^ flipped(m, A), b)

    def across(device):
        return (1 - c, device[1], device[2])

    def over(count, partner, both, action):
        def one(m, carry):
            device = partner(m)
            action(device)
            if both:
                action(across(device))
            return carry

        lax.fori_loop(0, count - 1, one, 0)
        if both:
            action(other)

    z_partners, cz_partners = (B, z_partner, False), (B, z_partner, True)
    xy_partners, cxy_partners = (A, xy_partner, False), (A, xy_partner, True)
    over(*cz_partners, signal)
    over(A, xy_partner, False, signal)
    over(A, lambda m: across(xy_partner(m)), False, signal)

    loads = [
        pltpu.make_async_copy(second_in, second_land, load_sem.at[0]),
        pltpu.make_async_copy(first_in, first_land, load_sem.at[1]),
    ]
    for load in loads:
        load.start()

    def load_cell(i):
        return pltpu.make_async_copy(contacts.at[i], x_full.at[i], load_sem.at[2 + i])

    for i in range(cells):
        load_cell(i).start()

    pad[...] = jnp.zeros_like(pad)
    loads[0].wait()
    pad[:width_second, :R] = second_land[...]
    packed = pack(pad[...].T[:R], SPREAD, lax.rem(width_second * in_cxy, 128))
    second_slots[in_cxy] = halve(packed, SPREAD // 2)
    loads[1].wait()
    pad[:width_first, :R] = first_land[...]
    packed = pack(pad[...].T[:R], SPREAD, lax.rem(width_first * in_cz, 128))
    first_slots[in_cz] = halve(packed, SPREAD // 2)

    def send(source, target, number, device):
        pltpu.make_async_remote_copy(
            source, target, send_sem.at[number], recv_sem.at[number], device_id=device, device_id_type=MESH
        ).start()

    def send_all(source, target, number, partners):
        over(*partners, lambda device: send(source, target, number, device))

    def arrived(like, number):
        pltpu.make_async_copy(like, like, recv_sem.at[number]).wait()

    def left(like, number):
        pltpu.make_async_copy(like, like, send_sem.at[number]).wait()

    def split_pair(p, carry):
        load_cell(2 * p).wait()
        load_cell(2 * p + 1).wait()
        pair = x_full[pl.ds(2 * p, 2)].reshape(2 * rows, columns)
        at = pl.ds(pl.multiple_of(2 * rows * p, 2 * rows), 2 * rows)
        high = pair.astype(jnp.bfloat16).astype(jnp.float32)
        low = pair - high
        half = columns // 2
        x_parts[at, :columns] = jnp.concatenate([high[:, :half], low[:, :half]], axis=1).astype(jnp.bfloat16)
        x_parts[at, columns:] = jnp.concatenate([high[:, half:], low[:, half:]], axis=1).astype(jnp.bfloat16)
        x_turned[:columns, at], x_turned[columns:, at] = split(pair.T)
        return carry

    pl.semaphore_wait(barrier, C * B - 1 + C * (A - 1))

    mine = second_slots.at[in_cxy]
    send_all(mine, mine, 0, cxy_partners)
    mine = first_slots.at[in_cz]
    send_all(mine, mine, 1, cz_partners)
    lax.fori_loop(0, cells // 2, split_pair, 0)

    arrived(second_slots.at[pl.ds(0, C * A - 1)], 0)
    second = spread(lambda v: two(second_slots, v), C * A, width_second, 3)
    second_rows = split_rows(jnp.concatenate(second, axis=1))
    second_rows = jnp.concatenate([second_rows, second_rows], axis=1)
    arrived(first_slots.at[pl.ds(0, C * B - 1)], 1)
    first = spread(lambda v: two(first_slots, v), C * B, width_first, 2)
    first_turned = [turn(group(first[0], q), 64) for q in range(G)]
    first_turned = stack(first_turned)
    last_turned = stack([turn(group(first[1], q), 64) for q in range(G)])
    first_pair = [
        first[0],
        jnp.where(lane24 < 64, first[1], first_turned),
        jnp.where(lane24 < 64, first_turned, last_turned),
    ]

    cell_terms = jnp.zeros((R, 128), jnp.float32)
    for p in range(cells // 2):
        if p % 2 == 0:
            at = pl.ds(2 * rows * p, 4 * rows)
            wide = jnp.dot(second_rows, x_turned[:, at], preferred_element_type=jnp.float32)
            wide = wide[:R] + wide[R:]
        both = wide[:, 2 * rows * (p % 2) : 2 * rows * (p % 2 + 1)]
        products[p] = both
        terms = [both[:, 128 * t : 128 * t + 128] * first_pair[t] for t in range(3)]
        even = jnp.sum(terms[0] + jnp.where(lane24 < 64, terms[1], 0.0), axis=1, keepdims=True)
        odd = jnp.sum(terms[2] + jnp.where(lane24 < 64, 0.0, terms[1]), axis=1, keepdims=True)
        cell_terms = jnp.where(lane24 == 2 * p, even, cell_terms)
        cell_terms = jnp.where(lane24 == 2 * p + 1, odd, cell_terms)

    terms_z[b] = pack(cell_terms, cells) + turn(pack(gram(second), R), 56)
    mine = terms_z.at[b]
    send_all(mine, mine, 2, z_partners)
    grams_xy[a] = pack(gram(first), R)
    mine = grams_xy.at[a]
    send_all(mine, mine, 3, xy_partners)

    arrived(terms_z.at[pl.ds(0, B - 1)], 2)
    summed = terms_z[0]
    for o in range(1, B):
        summed = summed + terms_z[o]
    terms_xy[in_cxy] = halve(jnp.where(lane8 < G * cells, summed, 0.0), G * cells)
    mine = terms_xy.at[in_cxy]
    send_all(mine, mine, 4, cxy_partners)

    gram_second = unpack(turn(summed, -56), R, R)
    arrived(grams_xy.at[pl.ds(0, A - 1)], 3)
    summed = grams_xy[0]
    for o in range(1, A):
        summed = summed + grams_xy[o]
    gram_first = unpack(summed, R, R)
    widen(inverse(gram_first * gram_second), wide_system)

    arrived(terms_xy.at[pl.ds(0, C * A - 1)], 4)
    cell_total = None
    for core in range(C):
        summed = terms_xy[core * A]
        for o in range(1, A):
            summed = summed + terms_xy[core * A + o]
        summed = jnp.concatenate([summed, summed], axis=0)
        block = unpack(jnp.where(upper8, summed, turn(summed, -G * cells)), cells, cells)
        block = stack([turn(group(block, q), cells * core) for q in range(G)])
        cell_total = block if cell_total is None else cell_total + block

    unscaled = apply(wide_system, cell_total)
    own_cells = stack([turn(group(unscaled, q), lax.rem(128 - cells * c, 128)) for q in range(G)])

    pair_sum = [jnp.zeros((R, 128), jnp.float32) for _ in range(3)]
    weights = []
    for p in range(cells // 2):
        even = jnp.broadcast_to(own_cells[:, 2 * p : 2 * p + 1], (R, 128))
        odd = jnp.broadcast_to(own_cells[:, 2 * p + 1 : 2 * p + 2], (R, 128))
        weight = [even, jnp.where(lane24 < 64, even, odd), odd]
        weights.append(weight)
        both = products[p]
        for t in range(3):
            pair_sum[t] = pair_sum[t] + both[:, 128 * t : 128 * t + 128] * weight[t]

    def half_turn(value):
        return stack([turn(group(value, q), 64) for q in range(G)])

    turned = [half_turn(pair_sum[1]), half_turn(pair_sum[2])]
    halves[0] = pair_sum[0] + jnp.where(lane24 < 64, turned[0], turned[1])
    halves[1] = jnp.where(lane24 < 64, pair_sum[1] + turned[1], 0.0)
    send(halves.at[1 - c], half_in, 5, other)

    arrived(half_in, 5)
    halves_z[b] = halves[c] + half_in[...]
    mine = halves_z.at[b]
    send_all(mine, mine, 6, z_partners)
    raw = gram([unscaled])
    scale_column, scale_row = diagonal_scales(raw, I)
    gram_cells = jnp.where(lane24 < R, raw / (scale_column * scale_row), 0.0)
    out[:cells, :] = flip(own_cells / scale_column)[:cells]
    cell_scales = scale_row
    widen(inverse(gram_cells * gram_second) / cell_scales, wide_system)
    arrived(halves_z.at[pl.ds(0, B - 1)], 6)
    summed = halves_z[0]
    for o in range(1, B):
        summed = summed + halves_z[o]
    solved[c] = apply(wide_system, summed)
    mine = solved.at[c]
    send(mine, mine, 7, other)
    arrived(solved.at[0], 7)
    low, high = solved[0], solved[1]
    raw_xy[a] = pack(gram([low, high]), R)

    low_turned, high_turned = half_turn(low), half_turn(high)
    solved_pair = [
        low,
        jnp.where(lane24 < 64, high, low_turned),
        jnp.where(lane24 < 64, low_turned, high_turned),
    ]
    for p in range(0, cells // 2, 2):
        left_rows[:, 2 * rows * p : 2 * rows * (p + 2)] = split_rows(
            jnp.concatenate([solved_pair[t] * weights[p + h][t] for h in range(2) for t in range(3)], axis=1)
        )

    def second_pass(core):
        at = pl.ds(pl.multiple_of(columns * core, columns), columns)
        total = None
        for p in range(0, cells // 2, 2):
            here = pl.ds(2 * rows * p, 4 * rows)
            both = jnp.dot(left_rows[:, here], x_parts[here, at], preferred_element_type=jnp.float32)
            total = both if total is None else total + both
        total = total[:R] + total[R:]
        first, middle, last = [total[:, 128 * t : 128 * t + 128] for t in range(3)]
        middle, last = half_turn(middle), half_turn(last)
        low = first + jnp.where(lane24 < 64, middle, last)
        high = jnp.where(lane24 < 64, total[:, 128:256] + last, 0.0)
        return jnp.concatenate([low, group(high, 0) + turn(group(high, 1), 64), group(high, 2)], axis=0)

    parts[...] = second_pass(1 - c)
    send(parts, part_in, 8, other)
    mine = raw_xy.at[a]
    send_all(mine, mine, 9, xy_partners)
    own_part = second_pass(c)
    arrived(part_in, 8)
    parts_xy[a] = own_part + part_in[...]
    mine = parts_xy.at[a]
    send_all(mine, mine, 10, xy_partners)

    arrived(raw_xy.at[pl.ds(0, A - 1)], 9)
    summed = raw_xy[0]
    for o in range(1, A):
        summed = summed + raw_xy[o]
    raw = unpack(summed, R, R)
    scale_column, scale_row = diagonal_scales(raw, J)
    gram_first = jnp.where(lane24 < R, raw / (scale_column * scale_row), 0.0)
    widen(inverse(gram_cells * gram_first) / scale_row / cell_scales, wide_system)
    start = width_first * in_cz
    at_low = lax.rem(256 - start, 128)
    piece = [
        jnp.where(lane8 < 128 - start, turn(group(solved[0], q), at_low), turn(group(solved[1], q), at_low))
        for q in range(G)
    ]
    out[cells : cells + width_first, :] = flip(stack(piece) / scale_column)[:width_first]

    arrived(parts_xy.at[pl.ds(0, A - 1)], 10)
    summed = parts_xy[0]
    for o in range(1, A):
        summed = summed + parts_xy[o]
    mixed = summed[R : R + 8]
    low = summed[:R]
    high = [jnp.where(lane8 < 64, mixed, 0.0), jnp.where(lane8 < 64, turn(mixed, 64), 0.0), summed[R + 8 :]]
    low, high = apply(wide_system, low), apply(wide_system, stack(high))

    norm = jnp.sum(low * low + high * high, axis=1, keepdims=True)
    row24 = lax.broadcasted_iota(jnp.int32, (R, 128), 0)
    norms[in_cz] = jnp.sum(jnp.where(lane24 == row24, norm, 0.0), axis=0, keepdims=True)
    mine = norms.at[in_cz]
    send_all(mine, mine, 11, cz_partners)
    start = width_second * a
    at_low = lax.rem(256 - start, 128)
    piece = [
        jnp.where(lane8 < 128 - start, turn(group(low, q), at_low), turn(group(high, q), at_low))
        for q in range(G)
    ]
    piece = flip(stack(piece))[:width_second]
    left(second_slots.at[pl.ds(0, C * A - 1)], 0)
    left(first_slots.at[pl.ds(0, C * B - 1)], 1)
    left(terms_z.at[pl.ds(0, B - 1)], 2)
    left(grams_xy.at[pl.ds(0, A - 1)], 3)
    left(terms_xy.at[pl.ds(0, C * A - 1)], 4)
    left(half_in, 5)
    left(halves_z.at[pl.ds(0, B - 1)], 6)
    left(solved.at[0], 7)
    left(part_in, 8)
    left(raw_xy.at[pl.ds(0, A - 1)], 9)
    left(parts_xy.at[pl.ds(0, A - 1)], 10)
    arrived(norms.at[pl.ds(0, C * B - 1)], 11)
    norm = norms[0]
    for o in range(1, C * B):
        norm = norm + norms[o]
    out[cells + 16 : cells + 16 + width_second, :] = piece / jnp.sqrt(norm / K + EPSILON)[:, :R]
    left(norms.at[pl.ds(0, C * B - 1)], 11)


def share(counts, out, cells, first, second, sem):
    copies = [
        pltpu.make_async_copy(out.at[pl.ds(16 * n, counts[n])], target, sem.at[n])
        for n, target in enumerate((cells, first, second))
    ]
    for copy in copies:
        copy.start()
    for copy in copies:
        copy.wait()


def per_device(sizes, contacts, first_bins, second_bins):
    C, A, B, I, J, K = sizes
    cells, rows, columns = contacts.shape
    f32 = jnp.float32

    def tiles(*lead):
        return pltpu.VMEM(lead + (8, 128), f32)

    first_bins, second_bins = first_bins.T, second_bins.T
    out = (
        pl.pallas_call(
            functools.partial(kernel, sizes),
            out_shape=jax.ShapeDtypeStruct((cells + 32, R), f32),
            in_specs=[pl.BlockSpec(memory_space=pl.ANY)] * 3,
            out_specs=pl.BlockSpec(memory_space=pltpu.VMEM),
            scratch_shapes=[
                pltpu.VMEM((cells, rows, columns), f32),
                pltpu.VMEM((cells * rows, 2 * columns), jnp.bfloat16),
                pltpu.VMEM((2 * columns, cells * rows), jnp.bfloat16),
                pltpu.VMEM(first_bins.shape, f32),
                pltpu.VMEM(second_bins.shape, f32),
                pltpu.VMEM((128, 128), f32),
                pltpu.VMEM((C * B, 4, 128), f32),
                pltpu.VMEM((C * A, 4, 128), f32),
                tiles(B),
                tiles(A),
                pltpu.VMEM((C * A, 4, 128), f32),
                pltpu.VMEM((cells // 2, R, 2 * rows), f32),
                pltpu.VMEM((2, R, 128), f32),
                pltpu.VMEM((R, 128), f32),
                pltpu.VMEM((B, R, 128), f32),
                pltpu.VMEM((2, R, 128), f32),
                tiles(A),
                pltpu.VMEM((2 * R, cells * rows), jnp.bfloat16),
                pltpu.VMEM((R + 16, 128), f32),
                pltpu.VMEM((R + 16, 128), f32),
                pltpu.VMEM((A, R + 16, 128), f32),
                pltpu.VMEM((C * B, 1, 128), f32),
                pltpu.VMEM((R, R, 128), f32),
                pltpu.SemaphoreType.DMA((2 + cells,)),
                pltpu.SemaphoreType.DMA((12,)),
                pltpu.SemaphoreType.DMA((12,)),
            ],
            compiler_params=pltpu.CompilerParams(
                collective_id=0, has_side_effects=True, vmem_limit_bytes=60 * 1024 * 1024
            ),
            name="sweep",
        )(contacts, first_bins, second_bins)
    )
    counts = (cells, first_bins.shape[0], second_bins.shape[0])
    shares = pl.pallas_call(
        functools.partial(share, counts),
        out_shape=tuple(jax.ShapeDtypeStruct((n, R), f32) for n in counts),
        in_specs=[pl.BlockSpec(memory_space=pltpu.VMEM)],
        out_specs=[pl.BlockSpec(memory_space=pl.ANY)] * 3,
        scratch_shapes=[pltpu.SemaphoreType.DMA((3,))],
        name="share",
    )(out)
    return tuple(piece.T for piece in shares)


def solution(mesh):
    placed = (
        P("cell", "bini", "binj"),
        P(None, ("bini", "cell", "binj")),
        P(None, ("binj", "cell", "bini")),
    )

    def whole(contacts, first_bins, second_bins):
        sizes = (
            mesh.shape["cell"],
            mesh.shape["bini"],
            mesh.shape["binj"],
            contacts.shape[0],
            first_bins.shape[1],
            second_bins.shape[1],
        )
        return jax.shard_map(
            functools.partial(per_device, sizes),
            mesh=mesh,
            in_specs=placed,
            out_specs=(
                P(None, "cell"),
                P(None, ("bini", "cell", "binj")),
                P(None, ("binj", "cell", "bini")),
            ),
            check_vma=False,
        )(contacts, first_bins, second_bins)

    return whole
```

```python
import functools

import jax
import jax.numpy as jnp
from jax import lax
from jax.experimental import pallas as pl
from jax.experimental.pallas import tpu as pltpu
from jax.sharding import PartitionSpec as P

EPSILON = 1e-06
PRECISE = lax.Precision.HIGHEST
MESH = pl.DeviceIdType.MESH
R = 24
G = 3
SPREAD = 40
NT = (((1,), (1,)), ((), ()))


def lanes(shape):
    return lax.broadcasted_iota(jnp.int32, shape, 1)


def group(value, q):
    return value[8 * q : 8 * q + 8, :]


def stack(tiles):
    return jnp.concatenate(tiles, axis=0)


def turn(value, shift):
    if isinstance(shift, int):
        shift = shift % 128
        return value if shift == 0 else pltpu.roll(value, shift, 1)
    return pltpu.roll(value, shift, 1)


def pack(value, step, base=None):
    out = None
    for q in range(G):
        if base is None:
            tile = turn(group(value, q), step * q)
        else:
            tile = turn(group(value, q), lax.rem(base + step * q, 128))
        out = tile if out is None else out + tile
    return out


def unpack(tile, step, width, base=None):
    parts = []
    for q in range(G):
        if base is None:
            part = turn(tile, -step * q)
        else:
            part = turn(tile, lax.rem(256 - base - step * q, 128))
        parts.append(jnp.where(lanes(part.shape) < width, part, 0.0))
    return stack(parts)


def within(lane, start, width):
    return ((lane - start) & 127) < width


def spread(tile_at, count, width, tiles):
    lane = lanes((8, 128))
    wholes = []
    for v in range(count // 2):
        wholes.extend(whole_pair(tile_at(v), SPREAD // 2))
    out = [[jnp.zeros((8, 128), jnp.float32) for _ in range(tiles)] for _ in range(G)]
    for o in range(count):
        tile = wholes[o]
        start = width * o
        for t in range(tiles):
            low, high = max(start, 128 * t), min(start + width, 128 * t + 128)
            if low >= high:
                continue
            for q in range(G):
                mask = within(lane, (low + SPREAD * q) % 128, high - low)
                out[q][t] = jnp.where(mask, tile, out[q][t])
    return [stack([turn(out[q][t], -SPREAD * q) for q in range(G)]) for t in range(tiles)]


def swap(tile):
    return pltpu.roll(tile, 4, 0)


def two(slots, v):
    return jnp.concatenate([slots[2 * v], slots[2 * v + 1]], axis=0)


def halve(tile, step):
    return (tile + turn(swap(tile), step))[:4]


def whole_pair(tile, step):
    upper = lax.broadcasted_iota(jnp.int32, (8, 128), 0) < 4
    swapped = swap(tile)
    return jnp.where(upper, tile, turn(swapped, -step)), jnp.where(upper, swapped, turn(tile, -step))


def flip(value):
    tall = jnp.concatenate([value, jnp.zeros((128 - R, 128), jnp.float32)], axis=0)
    return tall.T[:, :R]


def split(value):
    high = value.astype(jnp.bfloat16)
    return high, (value - high.astype(jnp.float32)).astype(jnp.bfloat16)


def split_rows(value):
    high = value.astype(jnp.bfloat16).astype(jnp.float32)
    return jnp.concatenate([high, value - high], axis=0).astype(jnp.bfloat16)


def gram(tiles):
    total = None
    for tile in tiles:
        tall = jnp.concatenate([tile, jnp.zeros((128 - R, 128), jnp.float32)], axis=0)
        part = lax.dot_general(tile, tall, NT, precision=PRECISE, preferred_element_type=jnp.float32)
        total = part if total is None else total + part
    return total


def inverse(a):
    lane, row = lanes((R, 128)), lax.broadcasted_iota(jnp.int32, (R, 128), 0)
    for k in range(R):
        pivot_row = a[k : k + 1, :]
        pivot_column = a[:, k : k + 1]
        over = 1.0 / a[k : k + 1, k : k + 1]
        new_row = jnp.where(lane[:1] == k, over, pivot_row * over)
        a = jnp.where(lane == k, 0.0, a) - pivot_column * new_row
        a = jnp.where(row == k, new_row, a)
    return a


def widen(matrix, wide):
    for s in range(R):
        wide[s] = jnp.broadcast_to(matrix[:, s : s + 1], (R, 128))


def apply(wide, value):
    total = None
    for s in range(R):
        term = wide[s] * value[s : s + 1, :]
        total = term if total is None else total + term
    return total


def diagonal_scales(raw, count):
    lane, row = lanes((R, 128)), lax.broadcasted_iota(jnp.int32, (R, 128), 0)
    diagonal = jnp.where(lane == row, raw, 0.0)
    column = jnp.sum(diagonal, axis=1, keepdims=True)
    across = jnp.sum(diagonal, axis=0, keepdims=True)
    return jnp.sqrt(column / count + EPSILON), jnp.sqrt(across / count + EPSILON)


def kernel(
    sizes,
    contacts,
    first_in,
    second_in,
    out,
    x_full,
    x_parts,
    x_turned,
    first_land,
    second_land,
    pad,
    first_slots,
    second_slots,
    terms_z,
    grams_xy,
    terms_xy,
    products,
    halves,
    half_in,
    halves_z,
    solved,
    raw_xy,
    left_rows,
    parts,
    part_in,
    parts_xy,
    norms,
    wide_system,
    load_sem,
    send_sem,
    recv_sem,
):
    C, A, B, I, J, K = sizes
    cells, rows, columns = x_full.shape
    width_first, width_second = rows // (C * B), x_full.shape[2] // (C * A)
    c, a, b = lax.axis_index("cell"), lax.axis_index("bini"), lax.axis_index("binj")
    in_cz, in_cxy = c * B + b, c * A + a
    other = (1 - c, a, b)
    lane8, lane24 = lanes((8, 128)), lanes((R, 128))
    upper8 = lax.broadcasted_iota(jnp.int32, (8, 128), 0) < 4

    barrier = pltpu.get_barrier_semaphore()

    def signal(device):
        pl.semaphore_signal(barrier, inc=1, device_id=device, device_id_type=MESH)

    def flipped(m, size):
        first = size // 2 if size == B else size // 2 + size // 8
        m = m + first
        return jnp.where(m >= size, m - size + 1, m)

    def z_partner(m):
        return (c, a, b ^ flipped(m, B))

    def xy_partner(m):
        return (c, a ^ flipped(m, A), b)

    def across(device):
        return (1 - c, device[1], device[2])

    def over(count, partner, both, action):
        def one(m, carry):
            device = partner(m)
            if both:
                action(across(device))
            action(device)
            return carry

        lax.fori_loop(0, count - 1, one, 0)
        if both:
            action(other)

    z_partners, cz_partners = (B, z_partner, False), (B, z_partner, True)
    xy_partners, cxy_partners = (A, xy_partner, False), (A, xy_partner, True)
    over(*cz_partners, signal)
    over(A, xy_partner, False, signal)
    over(A, lambda m: across(xy_partner(m)), False, signal)

    loads = [
        pltpu.make_async_copy(second_in, second_land, load_sem.at[0]),
        pltpu.make_async_copy(first_in, first_land, load_sem.at[1]),
    ]
    for load in loads:
        load.start()

    def load_cell(i):
        return pltpu.make_async_copy(contacts.at[i], x_full.at[i], load_sem.at[2 + i])

    for i in range(cells):
        load_cell(i).start()

    pad[...] = jnp.zeros_like(pad)
    loads[0].wait()
    pad[:width_second, :R] = second_land[...]
    packed = pack(pad[...].T[:R], SPREAD, lax.rem(width_second * in_cxy, 128))
    second_slots[in_cxy] = halve(packed, SPREAD // 2)
    loads[1].wait()
    pad[:width_first, :R] = first_land[...]
    packed = pack(pad[...].T[:R], SPREAD, lax.rem(width_first * in_cz, 128))
    first_slots[in_cz] = halve(packed, SPREAD // 2)

    def send(source, target, number, device):
        pltpu.make_async_remote_copy(
            source, target, send_sem.at[number], recv_sem.at[number], device_id=device, device_id_type=MESH
        ).start()

    def send_all(source, target, number, partners):
        over(*partners, lambda device: send(source, target, number, device))

    def arrived(like, number):
        pltpu.make_async_copy(like, like, recv_sem.at[number]).wait()

    def left(like, number):
        pltpu.make_async_copy(like, like, send_sem.at[number]).wait()

    def split_pair(p, carry):
        load_cell(2 * p).wait()
        load_cell(2 * p + 1).wait()
        pair = x_full[pl.ds(2 * p, 2)].reshape(2 * rows, columns)
        at = pl.ds(pl.multiple_of(2 * rows * p, 2 * rows), 2 * rows)
        high = pair.astype(jnp.bfloat16).astype(jnp.float32)
        low = pair - high
        half = columns // 2
        x_parts[at, :columns] = jnp.concatenate([high[:, :half], low[:, :half]], axis=1).astype(jnp.bfloat16)
        x_parts[at, columns:] = jnp.concatenate([high[:, half:], low[:, half:]], axis=1).astype(jnp.bfloat16)
        x_turned[:columns, at], x_turned[columns:, at] = split(pair.T)
        return carry

    pl.semaphore_wait(barrier, C * B - 1 + C * (A - 1))

    mine = second_slots.at[in_cxy]
    send_all(mine, mine, 0, cxy_partners)
    mine = first_slots.at[in_cz]
    send_all(mine, mine, 1, cz_partners)
    lax.fori_loop(0, cells // 2, split_pair, 0)

    arrived(second_slots.at[pl.ds(0, C * A - 1)], 0)
    second = spread(lambda v: two(second_slots, v), C * A, width_second, 3)
    second_rows = split_rows(jnp.concatenate(second, axis=1))
    second_rows = jnp.concatenate([second_rows, second_rows], axis=1)
    arrived(first_slots.at[pl.ds(0, C * B - 1)], 1)
    first = spread(lambda v: two(first_slots, v), C * B, width_first, 2)
    first_turned = [turn(group(first[0], q), 64) for q in range(G)]
    first_turned = stack(first_turned)
    last_turned = stack([turn(group(first[1], q), 64) for q in range(G)])
    first_pair = [
        first[0],
        jnp.where(lane24 < 64, first[1], first_turned),
        jnp.where(lane24 < 64, first_turned, last_turned),
    ]

    cell_terms = jnp.zeros((R, 128), jnp.float32)
    for p in range(cells // 2):
        if p % 2 == 0:
            at = pl.ds(2 * rows * p, 4 * rows)
            wide = jnp.dot(second_rows, x_turned[:, at], preferred_element_type=jnp.float32)
            wide = wide[:R] + wide[R:]
        both = wide[:, 2 * rows * (p % 2) : 2 * rows * (p % 2 + 1)]
        products[p] = both
        terms = [both[:, 128 * t : 128 * t + 128] * first_pair[t] for t in range(3)]
        even = jnp.sum(terms[0] + jnp.where(lane24 < 64, terms[1], 0.0), axis=1, keepdims=True)
        odd = jnp.sum(terms[2] + jnp.where(lane24 < 64, 0.0, terms[1]), axis=1, keepdims=True)
        cell_terms = jnp.where(lane24 == 2 * p, even, cell_terms)
        cell_terms = jnp.where(lane24 == 2 * p + 1, odd, cell_terms)

    terms_z[b] = pack(cell_terms, cells) + turn(pack(gram(second), R), 56)
    mine = terms_z.at[b]
    send_all(mine, mine, 2, z_partners)
    grams_xy[a] = pack(gram(first), R)
    mine = grams_xy.at[a]
    send_all(mine, mine, 3, xy_partners)

    arrived(terms_z.at[pl.ds(0, B - 1)], 2)
    summed = terms_z[0]
    for o in range(1, B):
        summed = summed + terms_z[o]
    terms_xy[in_cxy] = halve(jnp.where(lane8 < G * cells, summed, 0.0), G * cells)
    mine = terms_xy.at[in_cxy]
    send_all(mine, mine, 4, cxy_partners)

    gram_second = unpack(turn(summed, -56), R, R)
    arrived(grams_xy.at[pl.ds(0, A - 1)], 3)
    summed = grams_xy[0]
    for o in range(1, A):
        summed = summed + grams_xy[o]
    gram_first = unpack(summed, R, R)
    widen(inverse(gram_first * gram_second), wide_system)

    arrived(terms_xy.at[pl.ds(0, C * A - 1)], 4)
    cell_total = None
    for core in range(C):
        summed = terms_xy[core * A]
        for o in range(1, A):
            summed = summed + terms_xy[core * A + o]
        summed = jnp.concatenate([summed, summed], axis=0)
        block = unpack(jnp.where(upper8, summed, turn(summed, -G * cells)), cells, cells)
        block = stack([turn(group(block, q), cells * core) for q in range(G)])
        cell_total = block if cell_total is None else cell_total + block

    unscaled = apply(wide_system, cell_total)
    scale = jnp.sqrt(jnp.sum(unscaled * unscaled, axis=1, keepdims=True) / I + EPSILON)
    cell_factor = unscaled / scale
    own_cells = stack([turn(group(cell_factor, q), lax.rem(128 - cells * c, 128)) for q in range(G)])

    pair_sum = [jnp.zeros((R, 128), jnp.float32) for _ in range(3)]
    weights = []
    for p in range(cells // 2):
        even = jnp.broadcast_to(own_cells[:, 2 * p : 2 * p + 1], (R, 128))
        odd = jnp.broadcast_to(own_cells[:, 2 * p + 1 : 2 * p + 2], (R, 128))
        weight = [even, jnp.where(lane24 < 64, even, odd), odd]
        weights.append(weight)
        both = products[p]
        for t in range(3):
            pair_sum[t] = pair_sum[t] + both[:, 128 * t : 128 * t + 128] * weight[t]

    def half_turn(value):
        return stack([turn(group(value, q), 64) for q in range(G)])

    turned = [half_turn(pair_sum[1]), half_turn(pair_sum[2])]
    halves[0] = pair_sum[0] + jnp.where(lane24 < 64, turned[0], turned[1])
    halves[1] = jnp.where(lane24 < 64, pair_sum[1] + turned[1], 0.0)
    send(halves.at[1 - c], half_in, 5, other)

    arrived(half_in, 5)
    halves_z[b] = halves[c] + half_in[...]
    mine = halves_z.at[b]
    send_all(mine, mine, 6, z_partners)
    raw = gram([unscaled])
    scale_column, scale_row = diagonal_scales(raw, I)
    gram_cells = jnp.where(lane24 < R, raw / (scale_column * scale_row), 0.0)
    out[:cells, :] = flip(own_cells)[:cells]
    widen(inverse(gram_cells * gram_second), wide_system)
    arrived(halves_z.at[pl.ds(0, B - 1)], 6)
    summed = halves_z[0]
    for o in range(1, B):
        summed = summed + halves_z[o]
    solved[c] = apply(wide_system, summed)
    mine = solved.at[c]
    send(mine, mine, 7, other)
    arrived(solved.at[0], 7)
    low, high = solved[0], solved[1]
    raw_xy[a] = pack(gram([low, high]), R)

    low_turned, high_turned = half_turn(low), half_turn(high)
    solved_pair = [
        low,
        jnp.where(lane24 < 64, high, low_turned),
        jnp.where(lane24 < 64, low_turned, high_turned),
    ]
    for p in range(0, cells // 2, 2):
        left_rows[:, 2 * rows * p : 2 * rows * (p + 2)] = split_rows(
            jnp.concatenate([solved_pair[t] * weights[p + h][t] for h in range(2) for t in range(3)], axis=1)
        )

    def second_pass(core):
        at = pl.ds(pl.multiple_of(columns * core, columns), columns)
        total = None
        for p in range(0, cells // 2, 2):
            here = pl.ds(2 * rows * p, 4 * rows)
            both = jnp.dot(left_rows[:, here], x_parts[here, at], preferred_element_type=jnp.float32)
            total = both if total is None else total + both
        total = total[:R] + total[R:]
        first, middle, last = [total[:, 128 * t : 128 * t + 128] for t in range(3)]
        middle, last = half_turn(middle), half_turn(last)
        low = first + jnp.where(lane24 < 64, middle, last)
        high = jnp.where(lane24 < 64, total[:, 128:256] + last, 0.0)
        return jnp.concatenate([low, group(high, 0) + turn(group(high, 1), 64), group(high, 2)], axis=0)

    parts[...] = second_pass(1 - c)
    send(parts, part_in, 8, other)
    mine = raw_xy.at[a]
    send_all(mine, mine, 9, xy_partners)
    own_part = second_pass(c)
    arrived(part_in, 8)
    parts_xy[a] = own_part + part_in[...]
    mine = parts_xy.at[a]
    send_all(mine, mine, 10, xy_partners)

    arrived(raw_xy.at[pl.ds(0, A - 1)], 9)
    summed = raw_xy[0]
    for o in range(1, A):
        summed = summed + raw_xy[o]
    raw = unpack(summed, R, R)
    scale_column, scale_row = diagonal_scales(raw, J)
    gram_first = jnp.where(lane24 < R, raw / (scale_column * scale_row), 0.0)
    widen(inverse(gram_cells * gram_first) / scale_row, wide_system)
    start = width_first * in_cz
    at_low = lax.rem(256 - start, 128)
    piece = [
        jnp.where(lane8 < 128 - start, turn(group(solved[0], q), at_low), turn(group(solved[1], q), at_low))
        for q in range(G)
    ]
    out[cells : cells + width_first, :] = flip(stack(piece) / scale_column)[:width_first]

    arrived(parts_xy.at[pl.ds(0, A - 1)], 10)
    summed = parts_xy[0]
    for o in range(1, A):
        summed = summed + parts_xy[o]
    mixed = summed[R : R + 8]
    low = summed[:R]
    high = [jnp.where(lane8 < 64, mixed, 0.0), jnp.where(lane8 < 64, turn(mixed, 64), 0.0), summed[R + 8 :]]
    low, high = apply(wide_system, low), apply(wide_system, stack(high))

    norm = jnp.sum(low * low + high * high, axis=1, keepdims=True)
    row24 = lax.broadcasted_iota(jnp.int32, (R, 128), 0)
    norms[in_cz] = jnp.sum(jnp.where(lane24 == row24, norm, 0.0), axis=0, keepdims=True)
    mine = norms.at[in_cz]
    send_all(mine, mine, 11, cz_partners)
    start = width_second * a
    at_low = lax.rem(256 - start, 128)
    piece = [
        jnp.where(lane8 < 128 - start, turn(group(low, q), at_low), turn(group(high, q), at_low))
        for q in range(G)
    ]
    piece = flip(stack(piece))[:width_second]
    arrived(norms.at[pl.ds(0, C * B - 1)], 11)
    norm = norms[0]
    for o in range(1, C * B):
        norm = norm + norms[o]
    out[cells + 16 : cells + 16 + width_second, :] = piece / jnp.sqrt(norm / K + EPSILON)[:, :R]

    left(second_slots.at[pl.ds(0, C * A - 1)], 0)
    left(first_slots.at[pl.ds(0, C * B - 1)], 1)
    left(terms_z.at[pl.ds(0, B - 1)], 2)
    left(grams_xy.at[pl.ds(0, A - 1)], 3)
    left(terms_xy.at[pl.ds(0, C * A - 1)], 4)
    left(half_in, 5)
    left(halves_z.at[pl.ds(0, B - 1)], 6)
    left(solved.at[0], 7)
    left(part_in, 8)
    left(raw_xy.at[pl.ds(0, A - 1)], 9)
    left(parts_xy.at[pl.ds(0, A - 1)], 10)
    left(norms.at[pl.ds(0, C * B - 1)], 11)


def share(counts, out, cells, first, second, sem):
    copies = [
        pltpu.make_async_copy(out.at[pl.ds(16 * n, counts[n])], target, sem.at[n])
        for n, target in enumerate((cells, first, second))
    ]
    for copy in copies:
        copy.start()
    for copy in copies:
        copy.wait()


def per_device(sizes, contacts, first_bins, second_bins):
    C, A, B, I, J, K = sizes
    cells, rows, columns = contacts.shape
    f32 = jnp.float32

    def tiles(*lead):
        return pltpu.VMEM(lead + (8, 128), f32)

    first_bins, second_bins = first_bins.T, second_bins.T
    out = (
        pl.pallas_call(
            functools.partial(kernel, sizes),
            out_shape=jax.ShapeDtypeStruct((cells + 32, R), f32),
            in_specs=[pl.BlockSpec(memory_space=pl.ANY)] * 3,
            out_specs=pl.BlockSpec(memory_space=pltpu.VMEM),
            scratch_shapes=[
                pltpu.VMEM((cells, rows, columns), f32),
                pltpu.VMEM((cells * rows, 2 * columns), jnp.bfloat16),
                pltpu.VMEM((2 * columns, cells * rows), jnp.bfloat16),
                pltpu.VMEM(first_bins.shape, f32),
                pltpu.VMEM(second_bins.shape, f32),
                pltpu.VMEM((128, 128), f32),
                pltpu.VMEM((C * B, 4, 128), f32),
                pltpu.VMEM((C * A, 4, 128), f32),
                tiles(B),
                tiles(A),
                pltpu.VMEM((C * A, 4, 128), f32),
                pltpu.VMEM((cells // 2, R, 2 * rows), f32),
                pltpu.VMEM((2, R, 128), f32),
                pltpu.VMEM((R, 128), f32),
                pltpu.VMEM((B, R, 128), f32),
                pltpu.VMEM((2, R, 128), f32),
                tiles(A),
                pltpu.VMEM((2 * R, cells * rows), jnp.bfloat16),
                pltpu.VMEM((R + 16, 128), f32),
                pltpu.VMEM((R + 16, 128), f32),
                pltpu.VMEM((A, R + 16, 128), f32),
                pltpu.VMEM((C * B, 1, 128), f32),
                pltpu.VMEM((R, R, 128), f32),
                pltpu.SemaphoreType.DMA((2 + cells,)),
                pltpu.SemaphoreType.DMA((12,)),
                pltpu.SemaphoreType.DMA((12,)),
            ],
            compiler_params=pltpu.CompilerParams(
                collective_id=0, has_side_effects=True, vmem_limit_bytes=60 * 1024 * 1024
            ),
            name="sweep",
        )(contacts, first_bins, second_bins)
    )
    counts = (cells, first_bins.shape[0], second_bins.shape[0])
    shares = pl.pallas_call(
        functools.partial(share, counts),
        out_shape=tuple(jax.ShapeDtypeStruct((n, R), f32) for n in counts),
        in_specs=[pl.BlockSpec(memory_space=pltpu.VMEM)],
        out_specs=[pl.BlockSpec(memory_space=pl.ANY)] * 3,
        scratch_shapes=[pltpu.SemaphoreType.DMA((3,))],
        name="share",
    )(out)
    return tuple(piece.T for piece in shares)


def solution(mesh):
    placed = (
        P("cell", "bini", "binj"),
        P(None, ("bini", "cell", "binj")),
        P(None, ("binj", "cell", "bini")),
    )

    def whole(contacts, first_bins, second_bins):
        sizes = (
            mesh.shape["cell"],
            mesh.shape["bini"],
            mesh.shape["binj"],
            contacts.shape[0],
            first_bins.shape[1],
            second_bins.shape[1],
        )
        return jax.shard_map(
            functools.partial(per_device, sizes),
            mesh=mesh,
            in_specs=placed,
            out_specs=(
                P(None, "cell"),
                P(None, ("bini", "cell", "binj")),
                P(None, ("binj", "cell", "bini")),
            ),
            check_vma=False,
        )(contacts, first_bins, second_bins)

    return whole
```
